256 devices in a mesh: win: 4 (over y), space: 64 (over z, x, core).
Axes of the slice: x: 4, y: 4, z: 8, core: 2. Of those that a mesh axis runs over, the one named last changes fastest.
Arguments:
- multipliers: float32 [8, 12, 512, 256], P('win', None, 'space'), may hold values from -6 to 6
- increments: float32 [8, 12, 512, 256], P('win', None, 'space'), may hold values from -6 to 6
- background: float32 [8, 12, 512, 256], P('win', None, 'space'), may hold values from -1.8 to 2, as said below
- error_variance: float32 [8, 12, 512, 256], P('win', None, 'space'), may hold values from 0.25 to 4
- report_weights: float32 [8, 4, 16384], P('win', None, 'space'), may hold values from -6 to 6
- report_variance: float32 [8, 4, 16384], P('win', None, 'space'), may hold values from 0.25 to 4
- report_cells: int32 [8, 4, 16384], P('win', None, 'space'), may hold values from 0 to 24319, as said below
- report_offsets: float32 [8, 4, 2, 16384], P('win', None, None, 'space'), may hold values from 0 to 1
- report_counts: int32 [8, 4, 4096], P('win', None, 'space'), may hold values from 1 to 4, as said below
Outputs:
- model_residual: float32 [8, 12, 512, 256], P('win', None, 'space')
- report_residual: float32 [8, 4, 16384], P('win', None, 'space')
- adjoint_image: float32 [8, 12, 512, 256], P('win', None, 'space')
The draws below stay inside these ranges and needn't reach their ends.
Inputs may be any that keep to these rules, and one draw needn't show every extreme that they name: `report_cells`: entry p of slot s encodes channel c, strip row r below 7 and column q as p = c * 8 * 256 + r * 256 + q, the rows counted inside the slot's home strip. `report_counts`: entry m * 64 + o counts the live slots from home strip m to owner o at that step; they are the first ones of their 4. `background`: channels 3 l and 3 l + 1 hold velocities between -1.8 and 1.8; channel 3 l + 2 holds depths between 0.3 and 2.
All inputs are finite; a program needn't handle non-finite values.
Results may differ from the reference program's by a relative error of at most 0.0003.
Values sent between devices are 32-bit elements; how exact they have to be, the bound alone decides.
No kernel may reach another device: no remote copies, remote signals or barrier semaphores. Data moves between devices by JAX's collectives and lax.ppermute only.
A program may use at most 64 MiB of HBM per device.

```python
import math
import jax
import jax.numpy as jnp
import numpy as np
from jax import lax

NX = 256
RY = 8
STEPS = 4
LEVELS = 4
CAP = 4
CHANNELS = 12
SUBWIN = 8
NY = 512
PAIRS = 4096
SLOTS = 16384
N_SPACE = 64


def draw_background(key, part):
    key = jax.random.fold_in(key, 11)
    key_flow, key_depth = jax.random.split(key)
    shape_all = (SUBWIN, 3 * LEVELS, NY, NX)
    is_depth = (jnp.arange(3 * LEVELS) % 3 == 2)[None, :, None, None]
    velocity = 0.6 * jnp.clip(jax.random.normal(key_flow, shape_all, jnp.float32), -3.0, 3.0)
    depths = jax.random.uniform(key_depth, shape_all, jnp.float32, 0.5, 1.5)
    return jnp.where(is_depth, depths, velocity).astype(jnp.float32)


def draw_report_cells(key, part):
    key = jax.random.fold_in(key, 17)
    key_channel, key_row, key_column = jax.random.split(key, 3)
    shape_all = (SUBWIN, STEPS, SLOTS)
    channel = jax.random.randint(key_channel, shape_all, 0, 3 * LEVELS)
    row_place = jax.random.randint(key_row, shape_all, 0, RY - 1)
    column = jax.random.randint(key_column, shape_all, 0, NX)
    cells = channel * (RY * NX) + row_place * NX + column
    top_cell = 3 * LEVELS * RY * NX - NX - 1
    cells = cells.at[0, 0, 0].set(0).at[0, 0, 1].set(top_cell)
    return cells.astype(jnp.int32)


def draw_report_counts(key, part):
    key = jax.random.fold_in(key, 23)
    key_level, key_bits, key_place = jax.random.split(key, 3)
    strips = math.isqrt(PAIRS)
    strip_level = jax.random.randint(key_level, (1, 1, strips, 1), 2, CAP + 1)
    random_bits = jax.random.randint(key_bits, (SUBWIN, STEPS, strips, strips), 0, 1 << 20)
    counts = jnp.clip(strip_level - random_bits % 2, 1, CAP).reshape(SUBWIN, STEPS, PAIRS)
    forced_place = jax.random.randint(key_place, (), 0, PAIRS)
    return counts.at[0, 0, forced_place].set(CAP).astype(jnp.int32)


def block_scale(own_key, extent, cuts, smallest, high):
    factor_of = 1.0
    for axis_at, parts in cuts:
        draws = jax.random.uniform(jax.random.fold_in(jax.random.fold_in(own_key, 6), axis_at), (parts,), jnp.float32, smallest / len(cuts), high / len(cuts))
        factor_of = factor_of * jnp.repeat(jnp.exp(draws), extent[axis_at] // parts).reshape((-1,) + (1,) * (len(extent) - 1 - axis_at))
    return factor_of


def normal_values(own_key, shape, deviation, reach, cuts=(), kind=jnp.bfloat16):
    level = block_scale(own_key, shape, cuts, -0.22, 0.18) if cuts else 1.0
    values = jax.random.normal(own_key, shape, jnp.float32) * deviation * level
    return jnp.minimum(jnp.maximum(values, -reach), reach).astype(kind)


def setup_inputs(seed: int = 0) -> dict:
    key_of = jax.random.split(jax.random.key(seed), 10)
    multipliers = normal_values(key_of[0], (SUBWIN, CHANNELS, NY, NX), 1.0, 6.0, ((0, 4), (2, 64)), jnp.float32)
    increments = normal_values(key_of[1], (SUBWIN, CHANNELS, NY, NX), 1.0, 6.0, ((0, 4), (2, 64)), jnp.float32)
    background = draw_background(jax.random.fold_in(key_of[9], 71), 0)
    error_variance = jnp.clip(jnp.exp(math.log(4.0) - 2.7725887 * jax.random.uniform(key_of[3], (SUBWIN, CHANNELS, NY, NX), jnp.float32) ** block_scale(key_of[3], (SUBWIN, CHANNELS, NY, NX), ((0, 4), (2, 64)), -0.2, 0.2)), 0.25, 4.0)
    report_weights = normal_values(key_of[4], (SUBWIN, STEPS, SLOTS), 1.0, 6.0, ((0, 4), (2, 64)), jnp.float32)
    report_variance = jnp.clip(jnp.exp(math.log(4.0) - 2.7725887 * jax.random.uniform(key_of[5], (SUBWIN, STEPS, SLOTS), jnp.float32) ** block_scale(key_of[5], (SUBWIN, STEPS, SLOTS), ((0, 4), (2, 64)), -0.2, 0.2)), 0.25, 4.0)
    report_cells = draw_report_cells(jax.random.fold_in(key_of[9], 71), 0)
    report_offsets = jnp.clip(1.0 * jax.random.uniform(key_of[7], (SUBWIN, STEPS, 2, SLOTS), jnp.float32) ** block_scale(key_of[7], (SUBWIN, STEPS, 2, SLOTS), ((0, 4), (3, 64)), -0.2, 0.2), 0.0, 1.0)
    report_counts = draw_report_counts(jax.random.fold_in(key_of[9], 71), 0)
    return dict(multipliers=multipliers, increments=increments, background=background, error_variance=error_variance, report_weights=report_weights, report_variance=report_variance, report_cells=report_cells, report_offsets=report_offsets, report_counts=report_counts)


coupling = np.array([[1.0, 0.55, 0.3, 0.15], [0.5, 0.9, 0.45, 0.25], [0.3, 0.4, 0.8, 0.35], [0.1, 0.2, 0.35, 0.7]], np.float32)
time_step = 0.1
coriolis = 0.3
viscosity = 0.05

def across(field):
    return 0.5 * (jnp.roll(field, -1, axis=-1) - jnp.roll(field, 1, axis=-1))

def tendency(padded, backdrop):
    centre = padded[:, 1:-1]
    upper_rows = padded[:, 2:]
    lower_rows = padded[:, :-2]
    shaped = (centre.shape[0] // 3, 3, centre.shape[1], centre.shape[2])
    slope_rows = (0.5 * (upper_rows - lower_rows)).reshape(shaped)
    slope_cols = across(centre).reshape(shaped)
    smooth = (upper_rows + lower_rows + jnp.roll(centre, -1, axis=-1) + jnp.roll(centre, 1, axis=-1) - 4.0 * centre).reshape(shaped)
    fields = centre.reshape(shaped)
    speeds = backdrop.reshape(shaped)
    drift_cols = speeds[:, 0]
    drift_rows = speeds[:, 1]
    column_depth = speeds[:, 2]
    push_cols = jnp.einsum('lm,mrc->lrc', coupling, slope_cols[:, 2], precision=lax.Precision.HIGHEST)
    push_rows = jnp.einsum('lm,mrc->lrc', coupling, slope_rows[:, 2], precision=lax.Precision.HIGHEST)
    east_rate = -push_cols + coriolis * fields[:, 1] - drift_cols * slope_cols[:, 0] - drift_rows * slope_rows[:, 0] + viscosity * smooth[:, 0]
    north_rate = -push_rows - coriolis * fields[:, 0] - drift_cols * slope_cols[:, 1] - drift_rows * slope_rows[:, 1] + viscosity * smooth[:, 1]
    height_rate = -column_depth * (slope_cols[:, 0] + slope_rows[:, 1]) - drift_cols * slope_cols[:, 2] - drift_rows * slope_rows[:, 2] + viscosity * smooth[:, 2]
    return jnp.stack([east_rate, north_rate, height_rate], axis=1).reshape(centre.shape)

def advance(current, backdrop):
    padded = jnp.pad(current, ((0, 0), (1, 1), (0, 0)))
    return current + time_step * tendency(padded, backdrop)

def stencil(points, fractions, offset_rows, strip_rows, total_rows, grid_cols):
    plane_size = strip_rows * grid_cols
    channel = points // plane_size
    within = points % plane_size
    row_place = offset_rows + within // grid_cols
    column = within % grid_cols
    column_next = (column + 1) % grid_cols
    anchor = channel * (total_rows * grid_cols) + row_place * grid_cols
    indices = jnp.stack([anchor + column, anchor + column_next, anchor + grid_cols + column, anchor + grid_cols + column_next])
    share_cols = fractions[0]
    share_rows = fractions[1]
    weights = jnp.stack([(1.0 - share_cols) * (1.0 - share_rows), share_cols * (1.0 - share_rows), (1.0 - share_cols) * share_rows, share_cols * share_rows])
    return (indices, weights)

def swap_layout(values):
    blocks = values.reshape(values.shape[:-1] + (N_SPACE, N_SPACE, CAP))
    return jnp.swapaxes(blocks, -3, -2).reshape(values.shape)

def reference(multipliers, increments, background, error_variance, report_weights, report_variance, report_cells, report_offsets, report_counts):
    slot_index = jnp.arange(SLOTS, dtype=jnp.int32)
    home_strip = slot_index // (N_SPACE * CAP)
    offset_rows = home_strip * RY
    live_counts = jnp.repeat(report_counts, CAP, axis=-1)
    live_mask = (slot_index % CAP < live_counts).astype(jnp.float32)

    def forward_one(inputs):
        current, backdrop, points, fractions, masks = inputs
        sampled_list = []
        for moment in range(STEPS):
            indices, weights = stencil(points[moment], fractions[moment], offset_rows, RY, NY, NX)
            values = lax.optimization_barrier(jnp.sum(weights * current.reshape(-1)[indices], axis=0))
            sampled_list.append(values * masks[moment])
            current = advance(current, backdrop)
        return (current, jnp.stack(sampled_list))
    final_states, sampled = lax.map(forward_one, (increments, background, report_cells, report_offsets, live_mask))
    previous = jnp.concatenate([jnp.zeros_like(final_states[:1]), final_states[:-1]], axis=0)
    model_residual = error_variance * multipliers + increments - previous
    report_residual = report_variance * report_weights + swap_layout(sampled)
    home_weights = swap_layout(report_weights) * live_mask
    successors = jnp.concatenate([multipliers[1:], jnp.zeros_like(multipliers[:1])], axis=0)

    def backward_one(inputs):
        successor, backdrop, points, fractions, loads = inputs
        transpose = jax.vjp(lambda current: advance(current, backdrop), successor)[1]
        adjoint = -successor
        for moment in reversed(range(STEPS)):
            adjoint = transpose(adjoint)[0]
            indices, weights = stencil(points[moment], fractions[moment], offset_rows, RY, NY, NX)
            flattened = adjoint.reshape(-1).at[indices.reshape(-1)].add((weights * loads[moment]).reshape(-1))
            adjoint = flattened.reshape(adjoint.shape)
        return adjoint
    adjoints = lax.map(backward_one, (successors, background, report_cells, report_offsets, home_weights))
    adjoint_image = multipliers + adjoints
    return (model_residual, report_residual, adjoint_image)
```

```python
import jax
import jax.numpy as jnp
import numpy as np
from jax import lax
from jax.experimental import pallas as pl
from jax.experimental.pallas import tpu as pltpu
from jax.sharding import PartitionSpec as P

coupling = np.array(
    [[1.0, 0.55, 0.3, 0.15], [0.5, 0.9, 0.45, 0.25], [0.3, 0.4, 0.8, 0.35], [0.1, 0.2, 0.35, 0.7]],
    np.float32,
)
LEVELS = 4
VARS = 3
STEPS = 4
STRIP = 8
HALO = 4
EXT = STRIP + 2 * HALO
NX = 256
OWNERS = 64
CAP = 4
PARTS = 8
STATE_ROWS = VARS * STRIP * PARTS
FIELD_TILES = VARS * HALO
PACK = 3 * FIELD_TILES + 3

f32 = jnp.float32
bf16 = jnp.bfloat16
params = pltpu.CompilerParams(vmem_limit_bytes=48 * 2**20)


def east(z):
    return pltpu.roll(z, NX - 1, 1)


def west(z):
    return pltpu.roll(z, 1, 1)


def mix_weights(matrix):
    level = lax.broadcasted_iota(jnp.int32, (PARTS, NX), 0) % LEVELS
    weights = []
    for shift in range(1 - LEVELS, LEVELS):
        weight = jnp.zeros((PARTS, NX), f32)
        for l in range(LEVELS):
            if 0 <= l + shift < LEVELS:
                weight = jnp.where(level == l, float(matrix[l, l + shift]), weight)
        weights.append((shift, weight))
    return weights


def mix(z, weights):
    total = None
    for shift, weight in weights:
        term = weight * (z if shift == 0 else pltpu.roll(z, (-shift) % PARTS, 0))
        total = term if total is None else total + term
    return total


def split(x):
    high = x.astype(bf16)
    return high, (x - high.astype(f32)).astype(bf16)


def parity():
    return lax.axis_index("space") % 2 == 0


def state_rows(ref, v):
    return jnp.swapaxes(ref[:, v], 0, 1)


def owner_of_lane():
    lane = lax.broadcasted_iota(jnp.int32, (OWNERS, NX), 1)
    return lane // CAP == lax.broadcasted_iota(jnp.int32, (OWNERS, NX), 0)


def decode(report, k):
    p = report.astype(jnp.int32)
    channel = p >> 11
    level = (channel * 11) >> 5
    variable = channel - 3 * level
    code = (variable * STRIP + ((p >> 8) & 7)) * PARTS + level
    code = jnp.where(p < 0, -1024, code)
    return code + k * LEVELS, p & (NX - 1)


def one_hot_columns(column):
    place = lax.broadcasted_iota(jnp.int32, (NX, NX), 0)
    return jnp.where(place == column, 1.0, 0.0).astype(f32).astype(bf16)


def pack_kernel(inc, bg, mult, cells, offsets, counts, out_a, out_b, rep):
    even = parity()
    for f, ref in enumerate((inc, bg, mult)):
        for v in range(VARS):
            rows = state_rows(ref, v)
            low, high = rows[:HALO], rows[STRIP - HALO :]
            at = f * FIELD_TILES + v * HALO
            out_a[at : at + HALO] = jnp.where(even, high, low)
            out_b[at : at + HALO] = jnp.where(even, low, high)
    slot = lax.broadcasted_iota(jnp.int32, (PARTS, NX), 1) % CAP
    count = jnp.concatenate([counts[0], counts[1]], axis=0).astype(f32).astype(bf16)
    spread = jnp.where(owner_of_lane(), 1.0, 0.0).astype(f32).astype(bf16)
    live = slot.astype(f32) < jnp.dot(count, spread, preferred_element_type=f32)
    cell = jnp.concatenate([cells[0], cells[1]], axis=0).astype(f32)
    rep[0] = jnp.where(live, cell, -1.0)
    for k in range(2):
        for j in range(STEPS):
            for side in range(2):
                rep[1 + side, pl.ds(k * STEPS + j, 1), :] = offsets[k, j, pl.ds(side, 1), :]
    for n in range(3):
        out_a[3 * FIELD_TILES + n] = rep[n]
        out_b[3 * FIELD_TILES + n] = rep[n]


def tangent_kernel(
    inc, bg, mult, rep, got_a, got_b, owned, final0, final1, outer, send, state, back, raised, vals
):
    s = lax.axis_index("space")
    even = s % 2 == 0
    top = jnp.where(s > 0, 1.0, 0.0).astype(f32)
    bottom = jnp.where(s < OWNERS - 1, 1.0, 0.0).astype(f32)

    def halo_rows(f, v, i):
        at = f * FIELD_TILES + v * HALO + i
        a, b = got_a[at], got_b[at]
        return jnp.where(even, b, a), jnp.where(even, a, b)

    for v in range(VARS):
        for i in range(HALO):
            low, high = halo_rows(0, v, i)
            state[0, v, i] = low
            state[0, v, HALO + STRIP + i] = high
            low, high = halo_rows(1, v, i)
            back[v, i] = low
            back[v, HALO + STRIP + i] = high
        state[0, v, HALO : HALO + STRIP] = state_rows(inc, v)
        back[v, HALO : HALO + STRIP] = state_rows(bg, v)

    first = lax.broadcasted_iota(jnp.int32, (PARTS, NX), 0) < LEVELS
    for v in range(VARS):
        lows, highs = [], []
        for i in range(HALO):
            low, high = halo_rows(2, v, i)
            lows.append(low)
            highs.append(high)
        middle = state_rows(mult, v)
        rows = lows + [middle[r] for r in range(STRIP)] + highs
        for i in range(EXT // 2):
            outer[v * (EXT // 2) + i] = jnp.where(
                first, rows[i], pltpu.roll(rows[i + EXT // 2], LEVELS, 0)
            )

    weights = mix_weights(coupling)
    part = lax.broadcasted_iota(jnp.int32, (PARTS, NX), 0)
    cells = rep[0]
    for j in range(STEPS):
        now, later = j % 2, (j + 1) % 2
        x = jnp.concatenate(
            [state[now, v, HALO : HALO + STRIP].reshape(STRIP * PARTS, NX) for v in range(VARS)],
            axis=0,
        )
        high, low = split(x)
        high_e, low_e = split(east(x))
        stacked = jnp.concatenate([high, low, high_e, low_e], axis=0)
        for k in range(2):
            n = k * STEPS + j
            code, column = decode(cells[n : n + 1], k)
            picked = jnp.dot(stacked, one_hot_columns(column), preferred_element_type=f32)
            sums = [jnp.zeros((PARTS, NX), f32) for _ in range(4)]
            for v in range(VARS):
                before = None
                for r in range(STRIP):
                    at = (v * STRIP + r) * PARTS
                    here = code == part + at
                    t0 = picked[at : at + PARTS] + picked[STATE_ROWS + at : STATE_ROWS + at + PARTS]
                    t1 = (
                        picked[2 * STATE_ROWS + at : 2 * STATE_ROWS + at + PARTS]
                        + picked[3 * STATE_ROWS + at : 3 * STATE_ROWS + at + PARTS]
                    )
                    sums[0] = jnp.where(here, t0, sums[0])
                    sums[1] = jnp.where(here, t1, sums[1])
                    if before is not None:
                        sums[2] = jnp.where(before, t0, sums[2])
                        sums[3] = jnp.where(before, t1, sums[3])
                    before = here
            a, b = rep[1, n : n + 1], rep[2, n : n + 1]
            value = (1.0 - b) * ((1.0 - a) * sums[0] + a * sums[1]) + b * (
                (1.0 - a) * sums[2] + a * sums[3]
            )
            vals[pl.ds(n, 1), :] = jnp.sum(value, axis=0, keepdims=True)
        for row in range(j, EXT - j):
            raised[row] = mix(state[now, 2, row], weights)
        for row in range(j + 1, EXT - 1 - j):
            ub, vb, hb = back[0, row], back[1, row], back[2, row]
            centre = [state[now, v, row] for v in range(VARS)]
            up = [state[now, v, row + 1] for v in range(VARS)]
            down = [state[now, v, row - 1] for v in range(VARS)]
            e = [east(z) for z in centre]
            w = [west(z) for z in centre]
            cols = [e[v] - w[v] for v in range(VARS)]
            rows = [up[v] - down[v] for v in range(VARS)]
            smooth = [up[v] + down[v] + (e[v] + w[v]) for v in range(VARS)]
            lift = raised[row]
            push_c = east(lift) - west(lift)
            push_r = raised[row + 1] - raised[row - 1]
            ub, vb, hb = 0.05 * ub, 0.05 * vb, 0.05 * hb
            new = [
                0.98 * centre[0]
                + 0.03 * centre[1]
                + 0.005 * smooth[0]
                - 0.05 * push_c
                - (ub * cols[0] + vb * rows[0]),
                0.98 * centre[1]
                - 0.03 * centre[0]
                + 0.005 * smooth[1]
                - 0.05 * push_r
                - (ub * cols[1] + vb * rows[1]),
                0.98 * centre[2]
                + 0.005 * smooth[2]
                - hb * (cols[0] + rows[1])
                - (ub * cols[2] + vb * rows[2]),
            ]
            for v in range(VARS):
                value = new[v]
                if row < HALO:
                    value = value * top
                elif row >= HALO + STRIP:
                    value = value * bottom
                state[later, v, row] = value
    last = STEPS % 2
    for v in range(VARS):
        value = jnp.swapaxes(state[last, v, HALO : HALO + STRIP], 0, 1)
        final0[:, v] = value[:LEVELS]
        final1[:, v] = value[LEVELS:]
    own = jnp.concatenate([owned[0], owned[1]], axis=0)
    slot = lax.broadcasted_iota(jnp.int32, (PARTS, NX), 1) % CAP
    pieces = []
    for piece in (pltpu.roll(own, CAP, 1), own, pltpu.roll(own, NX - CAP, 1), vals[...]):
        for i in range(CAP):
            pieces.append(jnp.where(slot == i, piece, 0.0))
    chosen = jnp.where(owner_of_lane(), 1.0, 0.0).astype(f32)
    send[...] = lax.dot_general(
        chosen,
        jnp.concatenate(pieces, axis=0),
        (((1,), (1,)), ((), ())),
        precision=lax.Precision.HIGHEST,
        preferred_element_type=f32,
    )


def adjoint_kernel(
    mult,
    bg,
    variance,
    inc,
    rep,
    got_a,
    got_b,
    outer,
    final0,
    incoming,
    got,
    owned,
    owned_variance,
    model_out,
    report_out,
    image_out,
    state,
    back,
    flux,
):
    s = lax.axis_index("space")
    even = s % 2 == 0
    top = jnp.where(s > 0, 1.0, 0.0).astype(f32)
    bottom = jnp.where(s < OWNERS - 1, 1.0, 0.0).astype(f32)
    for part, before in ((slice(0, LEVELS), incoming), (slice(LEVELS, PARTS), final0)):
        model_out[part] = variance[part] * mult[part] + inc[part] - before[...]

    chosen = jnp.where(owner_of_lane(), 1.0, 0.0).astype(f32)
    spread = lax.dot_general(
        jnp.transpose(got[...]),
        chosen,
        (((1,), (0,)), ((), ())),
        precision=lax.Precision.HIGHEST,
        preferred_element_type=f32,
    )
    slot = lax.broadcasted_iota(jnp.int32, (PARTS, NX), 1) % CAP
    loads = []
    for g in range(4):
        value = jnp.zeros((PARTS, NX), f32)
        for i in range(CAP):
            at = (g * CAP + i) * PARTS
            value = jnp.where(slot == i, spread[at : at + PARTS], value)
        loads.append(value)
    for k in range(2):
        report_out[k] = (
            owned_variance[k] * owned[k] + loads[3][k * STEPS : (k + 1) * STEPS]
        )

    def halo_rows(f, v, i):
        at = f * FIELD_TILES + v * HALO + i
        a, b = got_a[at], got_b[at]
        return jnp.where(even, b, a), jnp.where(even, a, b)

    first = lax.broadcasted_iota(jnp.int32, (PARTS, NX), 0) < LEVELS
    for v in range(VARS):
        lows, highs = [], []
        for i in range(HALO):
            low, high = halo_rows(1, v, i)
            back[v, i] = low
            back[v, HALO + STRIP + i] = high
            low, high = halo_rows(2, v, i)
            lows.append(low)
            highs.append(high)
        back[v, HALO : HALO + STRIP] = state_rows(bg, v)
        middle = state_rows(mult, v)
        rows = lows + [middle[r] for r in range(STRIP)] + highs
        for i in range(EXT):
            after = outer[v * (EXT // 2) + i % (EXT // 2)]
            if i < EXT // 2:
                after = pltpu.roll(after, LEVELS, 0)
            state[0, v, i] = -jnp.where(first, pltpu.roll(rows[i], LEVELS, 0), after)

    reports = []
    base = 3 * FIELD_TILES
    for n in range(3):
        a, b = got_a[base + n], got_b[base + n]
        reports.append((jnp.where(even, b, a), rep[n], jnp.where(even, a, b)))
    part = lax.broadcasted_iota(jnp.int32, (PARTS, NX), 0)

    def field(side, j, rows):
        lhs, rhs = [], []
        for k in range(2):
            n = k * STEPS + j
            code, column = decode(reports[0][side][n : n + 1], k)
            a, b = reports[1][side][n : n + 1], reports[2][side][n : n + 1]
            load = loads[side][n : n + 1]
            parts = []
            for share in ((1.0 - a) * load, a * load):
                own, following = (1.0 - b) * share, b * share
                tiles = []
                for v in range(VARS):
                    for r in rows:
                        at = (v * STRIP + r) * PARTS
                        tile = jnp.where(code == part + at, own, 0.0)
                        if r > 0:
                            tile = jnp.where(code == part + (at - PARTS), following, tile)
                        tiles.append(tile)
                parts += list(split(jnp.concatenate(tiles, axis=0)))
            lhs.append(jnp.concatenate(parts, axis=0))
            rhs.append(one_hot_columns(column))
        out = lax.dot_general(
            jnp.concatenate(lhs, axis=1),
            jnp.concatenate(rhs, axis=1),
            (((1,), (1,)), ((), ())),
            preferred_element_type=f32,
        )
        count = VARS * len(rows) * PARTS
        total = out[:count] + out[count : 2 * count]
        total = total + west(out[2 * count : 3 * count] + out[3 * count :])
        tiles = {}
        for v in range(VARS):
            for at, r in enumerate(rows):
                first_row = (v * len(rows) + at) * PARTS
                tiles[v, r] = total[first_row : first_row + PARTS]
        return tiles

    weights = mix_weights(coupling.T)
    for step, j in enumerate(reversed(range(STEPS))):
        now, later = step % 2, (step + 1) % 2
        added = {}
        for (v, r), tile in field(1, j, list(range(STRIP))).items():
            added[v, HALO + r] = tile
        if j > 0:
            for (v, r), tile in field(0, j, list(range(STRIP - j, STRIP))).items():
                added[v, HALO + r - STRIP] = tile
            for (v, r), tile in field(2, j, list(range(j))).items():
                added[v, HALO + r + STRIP] = tile
        for row in range(step, EXT - step):
            ub, vb, hb = back[0, row], back[1, row], back[2, row]
            au, av, ah = state[now, 0, row], state[now, 1, row], state[now, 2, row]
            flux[0, row] = vb * au
            flux[1, row] = hb * ah + vb * av
            flux[2, row] = vb * ah + mix(av, weights)
        for row in range(step + 1, EXT - 1 - step):
            ub, vb, hb = back[0, row], back[1, row], back[2, row]
            centre = [state[now, v, row] for v in range(VARS)]
            au, av, ah = centre
            across = [hb * ah + ub * au, ub * av, ub * ah + mix(au, weights)]
            turn = [0.98 * au - 0.03 * av, 0.98 * av + 0.03 * au, 0.98 * ah]
            for v in range(VARS):
                near = (
                    state[now, v, row + 1]
                    + state[now, v, row - 1]
                    + (east(centre[v]) + west(centre[v]))
                )
                value = (
                    turn[v]
                    + 0.005 * near
                    + 0.05
                    * (
                        (east(across[v]) - west(across[v]))
                        + (flux[v, row + 1] - flux[v, row - 1])
                    )
                    + added[v, row]
                )
                if row < HALO:
                    value = value * top
                elif row >= HALO + STRIP:
                    value = value * bottom
                state[later, v, row] = value
    last = STEPS % 2
    for v in range(VARS):
        value = jnp.swapaxes(state[last, v, HALO : HALO + STRIP], 0, 1)
        image_out[:, v] = mult[:, v] + value


def vmem(count):
    return [pl.BlockSpec(memory_space=pltpu.VMEM)] * count


def shaped(*shape):
    return jax.ShapeDtypeStruct(shape, f32)


def per_device(
    multipliers,
    increments,
    background,
    error_variance,
    report_weights,
    report_variance,
    report_cells,
    report_offsets,
    report_counts,
):
    mult, inc, bg, variance = (
        x.reshape(PARTS, VARS, STRIP, NX) for x in (multipliers, increments, background, error_variance)
    )
    count = lax.axis_size("space")
    wins = lax.axis_size("win")
    pack_a, pack_b, rep = pl.pallas_call(
        pack_kernel,
        name="pack",
        out_shape=(shaped(PACK, PARTS, NX), shaped(PACK, PARTS, NX), shaped(3, PARTS, NX)),
        in_specs=vmem(6),
        out_specs=vmem(3),
        compiler_params=params,
    )(inc, bg, mult, report_cells, report_offsets, report_counts)
    inner = [(i, i + 1) for i in range(0, count, 2)]
    outward = [(i, i + 1) for i in range(1, count - 1, 2)]
    both = lambda pairs: pairs + [(target, source) for source, target in pairs]
    got_b = lax.ppermute(pack_b, "space", both(outward))
    got_a = lax.ppermute(pack_a, "space", both(inner))
    final0, final1, outer, send = pl.pallas_call(
        tangent_kernel,
        name="tangent",
        out_shape=(
            shaped(LEVELS, VARS, STRIP, NX),
            shaped(LEVELS, VARS, STRIP, NX),
            shaped(VARS * EXT // 2, PARTS, NX),
            shaped(OWNERS, 4 * CAP * PARTS),
        ),
        in_specs=vmem(7),
        out_specs=vmem(4),
        scratch_shapes=[
            pltpu.VMEM((2, VARS, EXT, PARTS, NX), f32),
            pltpu.VMEM((VARS, EXT, PARTS, NX), f32),
            pltpu.VMEM((EXT, PARTS, NX), f32),
            pltpu.VMEM((PARTS, NX), f32),
        ],
        compiler_params=params,
    )(inc, bg, mult, rep, got_a, got_b, report_weights)
    outer = lax.ppermute(outer, "win", [(i + 1, i) for i in range(wins - 1)])
    got = lax.all_to_all(send, "space", split_axis=0, concat_axis=0, tiled=True)
    incoming = lax.ppermute(final1, "win", [(i, i + 1) for i in range(wins - 1)])
    model, report, image = pl.pallas_call(
        adjoint_kernel,
        name="adjoint",
        out_shape=(
            shaped(PARTS, VARS, STRIP, NX),
            shaped(2, STEPS, NX),
            shaped(PARTS, VARS, STRIP, NX),
        ),
        in_specs=vmem(13),
        out_specs=vmem(3),
        scratch_shapes=[
            pltpu.VMEM((2, VARS, EXT, PARTS, NX), f32),
            pltpu.VMEM((VARS, EXT, PARTS, NX), f32),
            pltpu.VMEM((VARS, EXT, PARTS, NX), f32),
        ],
        compiler_params=params,
    )(
        mult,
        bg,
        variance,
        inc,
        rep,
        got_a,
        got_b,
        outer,
        final0,
        incoming,
        got,
        report_weights,
        report_variance,
    )
    return model.reshape(multipliers.shape), report, image.reshape(multipliers.shape)


def solution(mesh):
    state = P("win", None, "space", None)
    slots = P("win", None, "space")
    return jax.shard_map(
        per_device,
        mesh=mesh,
        in_specs=(state, state, state, state, slots, slots, slots, P("win", None, None, "space"), slots),
        out_specs=(state, slots, state),
        check_vma=False,
    )
```

```python
import jax
import jax.numpy as jnp
import numpy as np
from jax import lax
from jax.experimental import pallas as pl
from jax.experimental.pallas import tpu as pltpu
from jax.sharding import PartitionSpec as P

coupling = np.array(
    [[1.0, 0.55, 0.3, 0.15], [0.5, 0.9, 0.45, 0.25], [0.3, 0.4, 0.8, 0.35], [0.1, 0.2, 0.35, 0.7]],
    np.float32,
)
LEVELS = 4
VARS = 3
STEPS = 4
STRIP = 8
HALO = 4
EXT = STRIP + 2 * HALO
NX = 256
OWNERS = 64
CAP = 4
PARTS = 8
FIELD_TILES = VARS * HALO
NEAR = FIELD_TILES + VARS * (HALO - 1)
OUTER = FIELD_TILES
REPORTS = OUTER + 2
FAR = REPORTS + 3
CODES = VARS * STRIP * LEVELS
TILES = CODES // 8
FIRST_FIELD = [VARS * sum(STRIP + 2 * i for i in range(j)) for j in range(STEPS + 1)]
FIELDS_COST = 2
OUTER_COST = 0.01
ADJOINT_COST = 30
f32 = jnp.float32
bf16 = jnp.bfloat16
params = pltpu.CompilerParams(vmem_limit_bytes=20 * 2**20)


def east(z):
    return pltpu.roll(z, NX - 1, 1)


def west(z):
    return pltpu.roll(z, 1, 1)


def mix_weights(matrix):
    level = lax.broadcasted_iota(jnp.int32, (PARTS, NX), 0) % LEVELS
    weights = []
    for shift in range(1 - LEVELS, LEVELS):
        weight = jnp.zeros((PARTS, NX), f32)
        for l in range(LEVELS):
            if 0 <= l + shift < LEVELS:
                weight = jnp.where(level == l, float(matrix[l, l + shift]), weight)
        weights.append((shift, weight))
    return weights


def mix(z, weights):
    total = None
    for shift, weight in weights:
        term = weight * (z if shift == 0 else pltpu.roll(z, (-shift) % PARTS, 0))
        total = term if total is None else total + term
    return total


def split(x):
    high = x.astype(bf16)
    return high, (x - high.astype(f32)).astype(bf16)


def parity():
    return lax.axis_index("space") % 2 == 0


def state_rows(block):
    return jnp.swapaxes(block, 0, 1)


def owner_of_lane():
    lane = lax.broadcasted_iota(jnp.int32, (OWNERS, NX), 1)
    return lane // CAP == lax.broadcasted_iota(jnp.int32, (OWNERS, NX), 0)


def decode(report):
    p = report.astype(jnp.int32)
    channel = p >> 11
    level = (channel * 11) >> 5
    variable = channel - 3 * level
    code = (variable * STRIP + ((p >> 8) & 7)) * LEVELS + level
    return jnp.where(p < 0, -1024, code), p & (NX - 1)


def column_weights(report, n):
    _, column = decode(report[0, n : n + 1])
    share = report[1, n : n + 1]
    place = lax.broadcasted_iota(jnp.int32, (NX, NX), 0)
    following = jnp.where(place == ((column + 1) & (NX - 1)), share, 0.0)
    return split(jnp.where(place == column, 1.0 - share, following))


def one_hot_columns(column):
    place = lax.broadcasted_iota(jnp.int32, (NX, NX), 0)
    return jnp.where(place == column, 1.0, 0.0).astype(f32).astype(bf16)


def lower_half():
    return lax.broadcasted_iota(jnp.int32, (PARTS, NX), 0) < LEVELS


def code_tiles(rows):
    return [v * STRIP // 2 + t for v in range(VARS) for t in range(rows[0] // 2, rows[-1] // 2 + 1)]


def window_tiles(pair):
    first = lower_half()
    one = jnp.where(first, pair[0], pltpu.roll(pair[1], LEVELS, 0))
    two = jnp.where(first, pltpu.roll(pair[0], LEVELS, 0), pair[1])
    return one, two


def chosen_rows(low_end, rows, first, last):
    return jnp.where(low_end, rows[first:last], rows[STRIP - last : STRIP - first])


def near_halo(low_end, inc_rows, bg_rows, out):
    for v in range(VARS):
        at = v * HALO
        out[at : at + HALO] = chosen_rows(low_end, inc_rows[v], 0, HALO)
        at = FIELD_TILES + v * (HALO - 1)
        out[at : at + HALO - 1] = chosen_rows(low_end, bg_rows[v], 0, HALO - 1)


def far_halo(low_end, mult_rows, bg_rows, rep, out):
    for v in range(VARS):
        at = v * HALO
        out[at : at + HALO] = chosen_rows(low_end, mult_rows[v], 0, HALO)
        if v > 0:
            at = OUTER + v - 1
            out[at : at + 1] = chosen_rows(low_end, bg_rows[v], HALO - 1, HALO)
    out[REPORTS:] = rep[...]


def pack_kernel(
    inc, bg, mult, cells, offsets, counts,
    near, inner, rep, inc_rows, bg_rows, mult_rows,
    raw, raw_cells, raw_offsets, raw_counts, sems,
):
    copies = []
    for n, (source, target) in enumerate(
        (
            (inc, raw.at[0]),
            (bg, raw.at[1]),
            (mult, raw.at[2]),
            (cells, raw_cells),
            (offsets, raw_offsets),
            (counts, raw_counts),
        )
    ):
        copies.append(pltpu.make_async_copy(source, target, sems.at[n]))
        copies[n].start()
    even = parity()
    odd = jnp.logical_not(even)
    for f, rows_out in enumerate((inc_rows, bg_rows, mult_rows)):
        copies[f].wait()
        for v in range(VARS):
            rows_out[v] = state_rows(raw[f, :, v])
    near_halo(even, inc_rows, bg_rows, near)
    near_halo(odd, inc_rows, bg_rows, inner)
    for copy in copies[3:]:
        copy.wait()
    slot = lax.broadcasted_iota(jnp.int32, (PARTS, NX), 1) % CAP
    count = jnp.concatenate([raw_counts[0], raw_counts[1]], axis=0).astype(f32).astype(bf16)
    spread = jnp.where(owner_of_lane(), 1.0, 0.0).astype(f32).astype(bf16)
    live = slot.astype(f32) < jnp.dot(count, spread, preferred_element_type=f32)
    cell = jnp.concatenate([raw_cells[0], raw_cells[1]], axis=0).astype(f32)
    rep[0] = jnp.where(live, cell, -1.0)
    for k in range(2):
        for j in range(STEPS):
            for side in range(2):
                rep[1 + side, pl.ds(k * STEPS + j, 1), :] = raw_offsets[k, j, pl.ds(side, 1), :]
    far_halo(odd, mult_rows, bg_rows, rep, inner.at[NEAR:])


def sample(rows, j, rep, weights, rests, vals):
    pairs = [
        window_tiles((rows[v][r], rows[v][r + 1])) for v in range(VARS) for r in range(0, STRIP, 2)
    ]
    place = lax.broadcasted_iota(jnp.int32, (PARTS, NX), 0)
    for k in range(2):
        n = k * STEPS + j
        high, low = split(jnp.concatenate([pair[k] for pair in pairs], axis=0))
        code, _ = decode(rep[0, n : n + 1])
        picked = jnp.dot(
            jnp.concatenate([high, low], axis=0), weights[n], preferred_element_type=f32
        )
        rest = jnp.dot(high, rests[n], preferred_element_type=f32)
        sums = [jnp.zeros((PARTS, NX), f32) for _ in range(2)]
        for t in range(TILES):
            at = t * 8
            value = picked[at : at + 8] + (picked[CODES + at : CODES + at + 8] + rest[at : at + 8])
            sums = [
                jnp.where(code == place + at, value, sums[0]),
                jnp.where(code == place + (at - LEVELS), value, sums[1]),
            ]
        b = rep[2, n : n + 1]
        value = (1.0 - b) * sums[0] + b * sums[1]
        vals[pl.ds(n, 1), :] = jnp.sum(value, axis=0, keepdims=True)


def prepare_kernel(inc_rows, bg_rows, mult_rows, rep, far, along, rests, vals):
    far_halo(parity(), mult_rows, bg_rows, rep, far)
    for n in range(2 * STEPS):
        along[n], rests[n] = column_weights(rep, n)
    vals[...] = jnp.zeros((PARTS, NX), f32)
    rows = [[inc_rows[v, r] for r in range(STRIP)] for v in range(VARS)]
    sample(rows, 0, rep, along, rests, vals)


def edges():
    s = lax.axis_index("space")
    top = jnp.where(s > 0, 1.0, 0.0).astype(f32)
    bottom = jnp.where(s < OWNERS - 1, 1.0, 0.0).astype(f32)
    return top, bottom


def both_sides(even, a, b):
    return jnp.where(even, b, a), jnp.where(even, a, b)


def send_out(vals, owned, owned_variance, expected, send, packed, sem):
    own = jnp.concatenate([owned[0], owned[1]], axis=0)
    expected[...] = own * jnp.concatenate([owned_variance[0], owned_variance[1]], axis=0)
    slot = lax.broadcasted_iota(jnp.int32, (PARTS, NX), 1) % CAP
    pieces = []
    for piece in (pltpu.roll(own, CAP, 1), own, pltpu.roll(own, NX - CAP, 1), vals[...]):
        for i in range(CAP):
            pieces.append(jnp.where(slot == i, piece, 0.0))
    chosen = jnp.where(owner_of_lane(), 1.0, 0.0).astype(f32).astype(bf16)
    both = lax.dot_general(
        chosen,
        jnp.concatenate(split(jnp.concatenate(pieces, axis=0)), axis=0),
        (((1,), (1,)), ((), ())),
        preferred_element_type=f32,
    )
    lanes = 4 * CAP * PARTS
    packed[...] = both[:, :lanes] + both[:, lanes:]
    copy = pltpu.make_async_copy(packed, send, sem)
    copy.start()
    return copy


def tangent_kernel(
    inc_rows, bg_rows, rep, along, rests, early, got_a, got_near, owned, owned_variance,
    final0, final1, send, expected, back,
    state, raised, vals, packed, sem,
):
    even = parity()
    top, bottom = edges()
    end = HALO + STRIP
    for v in range(VARS):
        at = v * HALO
        low, high = both_sides(even, got_a[at : at + HALO], got_near[at : at + HALO])
        state[0, v, :HALO] = low
        state[0, v, HALO:end] = inc_rows[v]
        state[0, v, end:] = high
        at = FIELD_TILES + v * (HALO - 1)
        low, high = both_sides(even, got_a[at : at + HALO - 1], got_near[at : at + HALO - 1])
        back[v, 1:HALO] = low
        back[v, HALO:end] = bg_rows[v]
        back[v, end : EXT - 1] = high
        back[v, 0] = jnp.zeros((PARTS, NX), f32)
        back[v, EXT - 1] = jnp.zeros((PARTS, NX), f32)

    weights = mix_weights(coupling)
    vals[...] = early[...]
    for j in range(STEPS):
        now, later = j % 2, (j + 1) % 2
        if j > 0:
            rows = [[state[now, v, HALO + r] for r in range(STRIP)] for v in range(VARS)]
            sample(rows, j, rep, along, rests, vals)
        if j == STEPS - 1:
            copy = send_out(vals, owned, owned_variance, expected, send, packed, sem)
        for row in range(j, EXT - j):
            raised[row] = mix(state[now, 2, row], weights)
        for row in range(j + 1, EXT - 1 - j):
            ub, vb, hb = back[0, row], back[1, row], back[2, row]
            centre = [state[now, v, row] for v in range(VARS)]
            up = [state[now, v, row + 1] for v in range(VARS)]
            down = [state[now, v, row - 1] for v in range(VARS)]
            e = [east(z) for z in centre]
            w = [west(z) for z in centre]
            cols = [e[v] - w[v] for v in range(VARS)]
            rows = [up[v] - down[v] for v in range(VARS)]
            smooth = [up[v] + down[v] + (e[v] + w[v]) for v in range(VARS)]
            lift = raised[row]
            push_c = east(lift) - west(lift)
            push_r = raised[row + 1] - raised[row - 1]
            ub, vb, hb = 0.05 * ub, 0.05 * vb, 0.05 * hb
            new = [
                0.98 * centre[0]
                + 0.03 * centre[1]
                + 0.005 * smooth[0]
                - 0.05 * push_c
                - (ub * cols[0] + vb * rows[0]),
                0.98 * centre[1]
                - 0.03 * centre[0]
                + 0.005 * smooth[1]
                - 0.05 * push_r
                - (ub * cols[1] + vb * rows[1]),
                0.98 * centre[2]
                + 0.005 * smooth[2]
                - hb * (cols[0] + rows[1])
                - (ub * cols[2] + vb * rows[2]),
            ]
            for v in range(VARS):
                value = new[v]
                if row < HALO:
                    value = value * top
                elif row >= HALO + STRIP:
                    value = value * bottom
                state[later, v, row] = value
    last = STEPS % 2
    for v in range(VARS):
        value = state_rows(state[last, v, HALO : HALO + STRIP])
        final0[:, v] = value[:LEVELS]
        final1[:, v] = value[LEVELS:]
    copy.wait()


def outer_kernel(mult_rows, inner, far, final1, out, final_out, mine, outermost, sides):
    even = parity()
    half = EXT // 2
    final_out[...] = final1[...]
    for v in range(VARS):
        at = v * HALO
        low, high = both_sides(
            even, inner[NEAR + at : NEAR + at + HALO], far[at : at + HALO]
        )
        rows = (
            [low[i] for i in range(HALO)]
            + [mult_rows[v, r] for r in range(STRIP)]
            + [high[i] for i in range(HALO)]
        )
        for i in range(half):
            n = v * half + i
            out[n], mine[n] = window_tiles((rows[i], rows[i + half]))
    for v in (1, 2):
        at = OUTER + v - 1
        outermost[v - 1, 0], outermost[v - 1, 1] = both_sides(even, inner[NEAR + at], far[at])
    for n in range(3):
        at = REPORTS + n
        sides[0, n], sides[1, n] = both_sides(even, inner[NEAR + at], far[at])


def adjoint_step(step, now, later, back, flux, weights, added):
    top, bottom = edges()
    for row in range(step, EXT - step):
        vb, hb = back(1, row), back(2, row)
        au, av, ah = now[0, row], now[1, row], now[2, row]
        flux[0, row] = vb * au
        flux[1, row] = hb * ah + vb * av
        flux[2, row] = vb * ah + mix(av, weights)
    for row in range(step + 1, EXT - 1 - step):
        ub, hb = back(0, row), back(2, row)
        centre = [now[v, row] for v in range(VARS)]
        au, av, ah = centre
        across = [hb * ah + ub * au, ub * av, ub * ah + mix(au, weights)]
        turn = [0.98 * au - 0.03 * av, 0.98 * av + 0.03 * au, 0.98 * ah]
        for v in range(VARS):
            near = now[v, row + 1] + now[v, row - 1] + (east(centre[v]) + west(centre[v]))
            value = (
                turn[v]
                + 0.005 * near
                + 0.05
                * ((east(across[v]) - west(across[v])) + (flux[v, row + 1] - flux[v, row - 1]))
            )
            value = value + added(v, row)
            if row < HALO:
                value = value * top
            elif row >= HALO + STRIP:
                value = value * bottom
            later[v, row] = value


def fields_kernel(got, expected, rep, sides, report_out, fields):
    chosen = jnp.where(owner_of_lane(), 1.0, 0.0).astype(f32).astype(bf16)
    spread = jnp.dot(
        jnp.concatenate(split(jnp.transpose(got[...])), axis=0),
        chosen,
        preferred_element_type=f32,
    )
    lanes = 4 * CAP * PARTS
    spread = spread[:lanes] + spread[lanes:]
    slot = lax.broadcasted_iota(jnp.int32, (PARTS, NX), 1) % CAP
    loads = []
    for g in range(4):
        value = jnp.zeros((PARTS, NX), f32)
        for i in range(CAP):
            at = (g * CAP + i) * PARTS
            value = jnp.where(slot == i, spread[at : at + PARTS], value)
        loads.append(value)
    for k in range(2):
        at = k * STEPS
        report_out[k] = expected[pl.ds(at, STEPS), :] + loads[3][at : at + STEPS]
    place = lax.broadcasted_iota(jnp.int32, (PARTS, NX), 0)
    first = lower_half()
    transposed = (((1,), (1,)), ((), ()))

    def field(report, load, j, rows):
        tiles = code_tiles(rows)
        count = 8 * len(tiles)
        windows = []
        for k in range(2):
            n = k * STEPS + j
            code, column = decode(report[0, n : n + 1])
            a, b = report[1, n : n + 1], report[2, n : n + 1]
            weight = load[n : n + 1]
            parts = []
            for share in ((1.0 - a) * weight, a * weight):
                own, following = (1.0 - b) * share, b * share
                block = []
                for t in tiles:
                    tile = jnp.where(code == place + (8 * t - LEVELS), following, 0.0)
                    block.append(jnp.where(code == place + 8 * t, own, tile))
                parts += list(split(jnp.concatenate(block, axis=0)))
            out = lax.dot_general(
                jnp.concatenate(parts, axis=0),
                one_hot_columns(column),
                transposed,
                preferred_element_type=f32,
            )
            total = out[:count] + out[count : 2 * count]
            total = total + west(out[2 * count : 3 * count] + out[3 * count :])
            windows.append(total)
        for at, t in enumerate(tiles):
            one, two = (w[8 * at : 8 * at + 8] for w in windows)
            v, r = t // (STRIP // 2), 2 * (t % (STRIP // 2))
            yield v, r, jnp.where(first, one, pltpu.roll(two, LEVELS, 0))
            yield v, r + 1, jnp.where(first, pltpu.roll(one, LEVELS, 0), two)

    for j in range(STEPS):
        base = FIRST_FIELD[j]
        for v, r, tile in field(rep, loads[1], j, list(range(STRIP))):
            fields[base + v * (STRIP + 2 * j) + j + r] = tile
        if j > 0:
            for v, r, tile in field(sides.at[0], loads[0], j, list(range(STRIP - j, STRIP))):
                if r >= STRIP - j:
                    fields[base + v * (STRIP + 2 * j) + j + r - STRIP] = tile
            for v, r, tile in field(sides.at[1], loads[2], j, list(range(j))):
                if r < j:
                    fields[base + v * (STRIP + 2 * j) + j + r + STRIP] = tile


def adjoint_kernel(
    mult, variance, inc, outer, final0, mine, outermost, back, fields, report,
    model_out, report_out, image_out, partial,
    state, flux, raw, model, image, sems,
):
    copies = []
    for n, (source, target) in enumerate(
        (
            (mult, raw.at[0]),
            (variance, raw.at[1]),
            (inc, raw.at[2]),
        )
    ):
        copies.append(pltpu.make_async_copy(source, target, sems.at[n]))
        copies[n].start()

    def backdrop(v, row):
        if v > 0 and row in (0, EXT - 1):
            return outermost[v - 1, 1 if row else 0]
        return back[v, row]

    report_copy = pltpu.make_async_copy(report, report_out, sems.at[5])
    report_copy.start()
    first = lower_half()
    half = EXT // 2
    for v in range(VARS):
        for i in range(half):
            own, after = mine[v * half + i], outer[v * half + i]
            state[0, v, i] = -jnp.where(first, own, pltpu.roll(after, LEVELS, 0))
            state[0, v, i + half] = -jnp.where(first, pltpu.roll(own, LEVELS, 0), after)
    weights = mix_weights(coupling.T)
    for step, j in enumerate(reversed(range(STEPS))):
        now, later = state.at[step % 2], state.at[(step + 1) % 2]

        def added(v, row):
            return fields[FIRST_FIELD[j] + v * (STRIP + 2 * j) + row - step - 1]

        adjoint_step(step, now, later, backdrop, flux, weights, added)
        if step == 1:
            for copy in copies:
                copy.wait()
            for c in range(LEVELS):
                at = c + LEVELS
                partial[c] = raw[1, c] * raw[0, c] + raw[2, c]
                model[c] = raw[1, at] * raw[0, at] + raw[2, at] - final0[c]
            model_copy = pltpu.make_async_copy(model, model_out.at[LEVELS:], sems.at[3])
            model_copy.start()
    last = STEPS % 2
    for v in range(VARS):
        image[:, v] = raw[0, :, v] + state_rows(state[last, v, HALO : HALO + STRIP])
    image_copy = pltpu.make_async_copy(image, image_out, sems.at[4])
    image_copy.start()
    model_copy.wait()
    report_copy.wait()
    image_copy.wait()


def residual_kernel(model_in, partial, incoming, model_out, first, sem):
    first[...] = partial[...] - incoming[...]
    copy = pltpu.make_async_copy(first, model_out.at[:LEVELS], sem)
    copy.start()
    copy.wait()


def vmem(count):
    return [pl.BlockSpec(memory_space=pltpu.VMEM)] * count


def hbm(count):
    return [pl.BlockSpec(memory_space=pltpu.HBM)] * count


def far_from_core(x):
    return pltpu.with_memory_space_constraint(x, pltpu.HBM)


def shaped(*shape, kind=f32):
    return jax.ShapeDtypeStruct(shape, kind)


def cost(kernel_us):
    return pl.CostEstimate(flops=int(kernel_us * 1e9), bytes_accessed=int(kernel_us * 3e6), transcendentals=0)


def per_device(
    multipliers,
    increments,
    background,
    error_variance,
    report_weights,
    report_variance,
    report_cells,
    report_offsets,
    report_counts,
):
    mult, inc, bg, variance = (
        x.reshape(PARTS, VARS, STRIP, NX)
        for x in (multipliers, increments, background, error_variance)
    )
    count = lax.axis_size("space")
    wins = lax.axis_size("win")
    tile = (PARTS, NX)
    rows = shaped(VARS, STRIP, *tile)
    extended = shaped(VARS, EXT, *tile)
    whole = shaped(PARTS, VARS, STRIP, NX)
    scratch = pltpu.VMEM(whole.shape, f32)
    near, inner, rep, inc_rows, bg_rows, mult_rows = pl.pallas_call(
        pack_kernel,
        name="pack",
        out_shape=(
            shaped(NEAR, *tile),
            shaped(NEAR + FAR, *tile),
            shaped(3, *tile),
            rows,
            rows,
            rows,
        ),
        in_specs=hbm(6),
        out_specs=vmem(6),
        scratch_shapes=[
            pltpu.VMEM((3, *whole.shape), f32),
            pltpu.VMEM(report_cells.shape, jnp.int32),
            pltpu.VMEM(report_offsets.shape, f32),
            pltpu.VMEM(report_counts.shape, jnp.int32),
            pltpu.SemaphoreType.DMA((6,)),
        ],
        compiler_params=params,
    )(
        *(
            far_from_core(x)
            for x in (inc, bg, mult, report_cells, report_offsets, report_counts)
        )
    )
    both = lambda pairs: pairs + [(target, source) for source, target in pairs]
    near = lax.ppermute(near, "space", both([(i, i + 1) for i in range(1, count - 1, 2)]))
    inner = lax.ppermute(inner, "space", both([(i, i + 1) for i in range(0, count, 2)]))
    hot = shaped(2 * STEPS, NX, NX, kind=bf16)
    far, along, rests, early = pl.pallas_call(
        prepare_kernel,
        name="prepare",
        out_shape=(shaped(FAR, *tile), hot, hot, shaped(*tile)),
        in_specs=vmem(4),
        out_specs=vmem(4),
        cost_estimate=cost(2),
        compiler_params=params,
    )(inc_rows, bg_rows, mult_rows, rep)
    far = lax.ppermute(far, "space", both([(i, i + 1) for i in range(1, count - 1, 2)]))
    final0, final1, send, expected, back = pl.pallas_call(
        tangent_kernel,
        name="tangent",
        out_shape=(
            shaped(LEVELS, VARS, STRIP, NX),
            shaped(LEVELS, VARS, STRIP, NX),
            shaped(OWNERS, 4 * CAP * PARTS),
            shaped(*tile),
            extended,
        ),
        in_specs=vmem(10),
        out_specs=vmem(2) + hbm(1) + vmem(2),
        scratch_shapes=[
            pltpu.VMEM((2, *extended.shape), f32),
            pltpu.VMEM((EXT, *tile), f32),
            pltpu.VMEM(tile, f32),
            pltpu.VMEM((OWNERS, 4 * CAP * PARTS), f32),
            pltpu.SemaphoreType.DMA,
        ],
        cost_estimate=cost(2),
        compiler_params=params,
    )(
        inc_rows, bg_rows, rep, along, rests, early, inner, near, report_weights, report_variance
    )
    got = lax.all_to_all(send, "space", split_axis=0, concat_axis=0, tiled=True)
    folded = shaped(VARS * EXT // 2, *tile)
    half = shaped(LEVELS, VARS, STRIP, NX)
    outer, final1, mine, outermost, sides = pl.pallas_call(
        outer_kernel,
        name="outer",
        out_shape=(
            folded, half, folded, shaped(2, 2, *tile), shaped(2, 3, *tile)
        ),
        in_specs=vmem(4),
        out_specs=vmem(5),
        cost_estimate=cost(OUTER_COST),
        compiler_params=params,
    )(mult_rows, inner, far, final1)
    incoming = lax.ppermute(final1, "win", [(i, i + 1) for i in range(wins - 1)])
    outer = lax.ppermute(outer, "win", [(i + 1, i) for i in range(wins - 1)])
    report, fields = pl.pallas_call(
        fields_kernel,
        name="fields",
        out_shape=(shaped(2, STEPS, NX), shaped(FIRST_FIELD[STEPS], *tile)),
        in_specs=vmem(4),
        out_specs=vmem(2),
        cost_estimate=cost(FIELDS_COST),
        compiler_params=params,
    )(got, expected, rep, sides)
    model, report, image, partial = pl.pallas_call(
        adjoint_kernel,
        name="adjoint",
        out_shape=(whole, shaped(2, STEPS, NX), whole, half),
        in_specs=hbm(3) + vmem(7),
        out_specs=hbm(3) + vmem(1),
        scratch_shapes=[
            pltpu.VMEM((2, *extended.shape), f32),
            pltpu.VMEM(extended.shape, f32),
            pltpu.VMEM((3, *whole.shape), f32),
            pltpu.VMEM(half.shape, f32),
            scratch,
            pltpu.SemaphoreType.DMA((6,)),
        ],
        cost_estimate=cost(ADJOINT_COST),
        compiler_params=params,
    )(
        *(far_from_core(x) for x in (mult, variance, inc)),
        outer, final0, mine, outermost, back, fields, report,
    )
    model = pl.pallas_call(
        residual_kernel,
        name="residual",
        out_shape=whole,
        in_specs=hbm(1) + vmem(2),
        out_specs=hbm(1)[0],
        input_output_aliases={0: 0},
        scratch_shapes=[pltpu.VMEM(half.shape, f32), pltpu.SemaphoreType.DMA],
        compiler_params=params,
    )(far_from_core(model), partial, incoming)
    return model.reshape(multipliers.shape), report, image.reshape(multipliers.shape)


def solution(mesh):
    state = P("win", None, "space", None)
    slots = P("win", None, "space")
    return jax.shard_map(
        per_device,
        mesh=mesh,
        in_specs=(state, state, state, state, slots, slots, slots, P("win", None, None, "space"), slots),
        out_specs=(state, slots, state),
        check_vma=False,
    )
```

```python
import jax
import jax.numpy as jnp
import numpy as np
from jax import lax
from jax.experimental import pallas as pl
from jax.experimental.pallas import tpu as pltpu
from jax.sharding import PartitionSpec as P

coupling = np.array(
    [[1.0, 0.55, 0.3, 0.15], [0.5, 0.9, 0.45, 0.25], [0.3, 0.4, 0.8, 0.35], [0.1, 0.2, 0.35, 0.7]],
    np.float32,
)
LEVELS = 4
VARS = 3
STEPS = 4
STRIP = 8
HALO = 4
EXT = STRIP + 2 * HALO
NX = 256
OWNERS = 64
CAP = 4
PARTS = 8
FIELD_TILES = VARS * HALO
NEAR = FIELD_TILES + VARS * (HALO - 1)
OUTER = FIELD_TILES
REPORTS = OUTER + 2
FAR = REPORTS + 3
CODES = VARS * STRIP * LEVELS
TILES = CODES // 8
FIRST_FIELD = [VARS * sum(STRIP + 2 * i for i in range(j)) for j in range(STEPS + 1)]
FIELDS_COST = 2
OUTER_COST = 0.01
ADJOINT_COST = 30
SCALE = 0.05
f32 = jnp.float32
bf16 = jnp.bfloat16
params = pltpu.CompilerParams(vmem_limit_bytes=20 * 2**20)


def east(z):
    return pltpu.roll(z, NX - 1, 1)


def west(z):
    return pltpu.roll(z, 1, 1)


def mix_weights(matrix):
    level = lax.broadcasted_iota(jnp.int32, (PARTS, NX), 0) % LEVELS
    weights = []
    for shift in range(1 - LEVELS, LEVELS):
        weight = jnp.zeros((PARTS, NX), f32)
        for l in range(LEVELS):
            if 0 <= l + shift < LEVELS:
                weight = jnp.where(level == l, float(matrix[l, l + shift]), weight)
        weights.append((shift, weight))
    return weights


def mix(z, weights):
    total = None
    for shift, weight in weights:
        term = weight * (z if shift == 0 else pltpu.roll(z, (-shift) % PARTS, 0))
        total = term if total is None else total + term
    return total


def split(x):
    high = x.astype(bf16)
    return high, (x - high.astype(f32)).astype(bf16)


def parity():
    return lax.axis_index("space") % 2 == 0


def state_rows(block):
    return jnp.swapaxes(block, 0, 1)


def owner_of_lane():
    lane = lax.broadcasted_iota(jnp.int32, (OWNERS, NX), 1)
    return lane // CAP == lax.broadcasted_iota(jnp.int32, (OWNERS, NX), 0)


def decode(report):
    p = report.astype(jnp.int32)
    channel = p >> 11
    level = (channel * 11) >> 5
    variable = channel - 3 * level
    code = (variable * STRIP + ((p >> 8) & 7)) * LEVELS + level
    return jnp.where(p < 0, -1024, code), p & (NX - 1)


def column_weights(report, n):
    _, column = decode(report[0, n : n + 1])
    share = report[1, n : n + 1]
    place = lax.broadcasted_iota(jnp.int32, (NX, NX), 0)
    following = jnp.where(place == ((column + 1) & (NX - 1)), share, 0.0)
    return split(jnp.where(place == column, 1.0 - share, following))


def one_hot_columns(column):
    place = lax.broadcasted_iota(jnp.int32, (NX, NX), 0)
    return jnp.where(place == column, 1.0, 0.0).astype(f32).astype(bf16)


def lower_half():
    return lax.broadcasted_iota(jnp.int32, (PARTS, NX), 0) < LEVELS


def code_tiles(rows):
    return [v * STRIP // 2 + t for v in range(VARS) for t in range(rows[0] // 2, rows[-1] // 2 + 1)]


def window_tiles(pair):
    first = lower_half()
    one = jnp.where(first, pair[0], pltpu.roll(pair[1], LEVELS, 0))
    two = jnp.where(first, pltpu.roll(pair[0], LEVELS, 0), pair[1])
    return one, two


def chosen_rows(low_end, rows, first, last):
    return jnp.where(low_end, rows[first:last], rows[STRIP - last : STRIP - first])


def near_halo(low_end, inc_rows, bg_rows, out):
    for v in range(VARS):
        at = v * HALO
        out[at : at + HALO] = chosen_rows(low_end, inc_rows[v], 0, HALO)
        at = FIELD_TILES + v * (HALO - 1)
        out[at : at + HALO - 1] = chosen_rows(low_end, bg_rows[v], 0, HALO - 1)


def far_halo(low_end, mult_rows, bg_rows, rep, out):
    for v in range(VARS):
        at = v * HALO
        out[at : at + HALO] = chosen_rows(low_end, mult_rows[v], 0, HALO)
        if v > 0:
            at = OUTER + v - 1
            out[at : at + 1] = chosen_rows(low_end, bg_rows[v], HALO - 1, HALO)
    out[REPORTS:] = rep[...]


def pack_kernel(
    inc, bg, mult, cells, offsets, counts,
    near, inner, rep, inc_rows, bg_rows, mult_rows,
    raw, raw_cells, raw_offsets, raw_counts, sems,
):
    copies = []
    for n, (source, target) in enumerate(
        (
            (inc, raw.at[0]),
            (bg, raw.at[1]),
            (mult, raw.at[2]),
            (cells, raw_cells),
            (offsets, raw_offsets),
            (counts, raw_counts),
        )
    ):
        copies.append(pltpu.make_async_copy(source, target, sems.at[n]))
        copies[n].start()
    even = parity()
    odd = jnp.logical_not(even)
    for f, rows_out in enumerate((inc_rows, bg_rows, mult_rows)):
        copies[f].wait()
        for v in range(VARS):
            rows_out[v] = state_rows(raw[f, :, v])
    near_halo(even, inc_rows, bg_rows, near)
    near_halo(odd, inc_rows, bg_rows, inner)
    for copy in copies[3:]:
        copy.wait()
    slot = lax.broadcasted_iota(jnp.int32, (PARTS, NX), 1) % CAP
    count = jnp.concatenate([raw_counts[0], raw_counts[1]], axis=0).astype(f32).astype(bf16)
    spread = jnp.where(owner_of_lane(), 1.0, 0.0).astype(f32).astype(bf16)
    live = slot.astype(f32) < jnp.dot(count, spread, preferred_element_type=f32)
    cell = jnp.concatenate([raw_cells[0], raw_cells[1]], axis=0).astype(f32)
    rep[0] = jnp.where(live, cell, -1.0)
    for k in range(2):
        for j in range(STEPS):
            for side in range(2):
                rep[1 + side, pl.ds(k * STEPS + j, 1), :] = raw_offsets[k, j, pl.ds(side, 1), :]
    far_halo(odd, mult_rows, bg_rows, rep, inner.at[NEAR:])


def sample(rows, j, rep, weights, rests, vals):
    pairs = [
        window_tiles((rows[v][r], rows[v][r + 1])) for v in range(VARS) for r in range(0, STRIP, 2)
    ]
    place = lax.broadcasted_iota(jnp.int32, (PARTS, NX), 0)
    for k in range(2):
        n = k * STEPS + j
        high, low = split(jnp.concatenate([pair[k] for pair in pairs], axis=0))
        code, _ = decode(rep[0, n : n + 1])
        picked = jnp.dot(
            jnp.concatenate([high, low], axis=0), weights[n], preferred_element_type=f32
        )
        rest = jnp.dot(high, rests[n], preferred_element_type=f32)
        sums = [jnp.zeros((PARTS, NX), f32) for _ in range(2)]
        for t in range(TILES):
            at = t * 8
            value = picked[at : at + 8] + (picked[CODES + at : CODES + at + 8] + rest[at : at + 8])
            sums = [
                jnp.where(code == place + at, value, sums[0]),
                jnp.where(code == place + (at - LEVELS), value, sums[1]),
            ]
        b = rep[2, n : n + 1]
        value = (1.0 - b) * sums[0] + b * sums[1]
        vals[pl.ds(n, 1), :] = jnp.sum(value, axis=0, keepdims=True)


def prepare_kernel(inc_rows, bg_rows, mult_rows, rep, far, along, rests, vals):
    far_halo(parity(), mult_rows, bg_rows, rep, far)
    for n in range(2 * STEPS):
        along[n], rests[n] = column_weights(rep, n)
    vals[...] = jnp.zeros((PARTS, NX), f32)
    rows = [[inc_rows[v, r] for r in range(STRIP)] for v in range(VARS)]
    sample(rows, 0, rep, along, rests, vals)


def edges():
    s = lax.axis_index("space")
    top = jnp.where(s > 0, 1.0, 0.0).astype(f32)
    bottom = jnp.where(s < OWNERS - 1, 1.0, 0.0).astype(f32)
    return top, bottom


def both_sides(even, a, b):
    return jnp.where(even, b, a), jnp.where(even, a, b)


def send_out(vals, owned, owned_variance, expected, send, packed, sem):
    own = jnp.concatenate([owned[0], owned[1]], axis=0)
    expected[...] = own * jnp.concatenate([owned_variance[0], owned_variance[1]], axis=0)
    slot = lax.broadcasted_iota(jnp.int32, (PARTS, NX), 1) % CAP
    pieces = []
    for piece in (pltpu.roll(own, CAP, 1), own, pltpu.roll(own, NX - CAP, 1), vals[...]):
        for i in range(CAP):
            pieces.append(jnp.where(slot == i, piece, 0.0))
    chosen = jnp.where(owner_of_lane(), 1.0, 0.0).astype(f32).astype(bf16)
    both = lax.dot_general(
        chosen,
        jnp.concatenate(split(jnp.concatenate(pieces, axis=0)), axis=0),
        (((1,), (1,)), ((), ())),
        preferred_element_type=f32,
    )
    lanes = 4 * CAP * PARTS
    packed[...] = both[:, :lanes] + both[:, lanes:]
    copy = pltpu.make_async_copy(packed, send, sem)
    copy.start()
    return copy


def tangent_kernel(
    inc_rows, bg_rows, rep, along, rests, early, got_a, got_near, owned, owned_variance,
    final0, final1, send, expected, back,
    state, raised, vals, packed, sem,
):
    even = parity()
    top, bottom = edges()
    end = HALO + STRIP
    for v in range(VARS):
        at = v * HALO
        low, high = both_sides(even, got_a[at : at + HALO], got_near[at : at + HALO])
        state[0, v, :HALO] = low
        state[0, v, HALO:end] = inc_rows[v]
        state[0, v, end:] = high
        at = FIELD_TILES + v * (HALO - 1)
        low, high = both_sides(even, got_a[at : at + HALO - 1], got_near[at : at + HALO - 1])
        back[v, 1:HALO] = SCALE * low
        back[v, HALO:end] = SCALE * bg_rows[v]
        back[v, end : EXT - 1] = SCALE * high
        back[v, 0] = jnp.zeros((PARTS, NX), f32)
        back[v, EXT - 1] = jnp.zeros((PARTS, NX), f32)

    weights = mix_weights(SCALE * coupling)
    vals[...] = early[...]
    for j in range(STEPS):
        now, later = j % 2, (j + 1) % 2
        if j > 0:
            rows = [[state[now, v, HALO + r] for r in range(STRIP)] for v in range(VARS)]
            sample(rows, j, rep, along, rests, vals)
        if j == STEPS - 1:
            copy = send_out(vals, owned, owned_variance, expected, send, packed, sem)
        for row in range(j, EXT - j):
            raised[row] = mix(state[now, 2, row], weights)
        for row in range(j + 1, EXT - 1 - j):
            ub, vb, hb = back[0, row], back[1, row], back[2, row]
            centre = [state[now, v, row] for v in range(VARS)]
            up = [state[now, v, row + 1] for v in range(VARS)]
            down = [state[now, v, row - 1] for v in range(VARS)]
            e = [east(z) for z in centre]
            w = [west(z) for z in centre]
            cols = [e[v] - w[v] for v in range(VARS)]
            rows = [up[v] - down[v] for v in range(VARS)]
            smooth = [up[v] + down[v] + (e[v] + w[v]) for v in range(VARS)]
            lift = raised[row]
            push_c = east(lift) - west(lift)
            push_r = raised[row + 1] - raised[row - 1]
            new = [
                0.98 * centre[0]
                + 0.03 * centre[1]
                + 0.005 * smooth[0]
                - push_c
                - (ub * cols[0] + vb * rows[0]),
                0.98 * centre[1]
                - 0.03 * centre[0]
                + 0.005 * smooth[1]
                - push_r
                - (ub * cols[1] + vb * rows[1]),
                0.98 * centre[2]
                + 0.005 * smooth[2]
                - hb * (cols[0] + rows[1])
                - (ub * cols[2] + vb * rows[2]),
            ]
            for v in range(VARS):
                value = new[v]
                if row < HALO:
                    value = value * top
                elif row >= HALO + STRIP:
                    value = value * bottom
                state[later, v, row] = value
    last = STEPS % 2
    for v in range(VARS):
        value = state_rows(state[last, v, HALO : HALO + STRIP])
        final0[:, v] = value[:LEVELS]
        final1[:, v] = value[LEVELS:]
    copy.wait()


def outer_kernel(mult_rows, inner, far, final1, out, final_out, mine, outermost, sides):
    even = parity()
    half = EXT // 2
    final_out[...] = final1[...]
    for v in range(VARS):
        at = v * HALO
        low, high = both_sides(
            even, inner[NEAR + at : NEAR + at + HALO], far[at : at + HALO]
        )
        rows = (
            [low[i] for i in range(HALO)]
            + [mult_rows[v, r] for r in range(STRIP)]
            + [high[i] for i in range(HALO)]
        )
        for i in range(half):
            n = v * half + i
            out[n], mine[n] = window_tiles((rows[i], rows[i + half]))
    for v in (1, 2):
        at = OUTER + v - 1
        low, high = both_sides(even, inner[NEAR + at], far[at])
        outermost[v - 1, 0], outermost[v - 1, 1] = SCALE * low, SCALE * high
    for n in range(3):
        at = REPORTS + n
        sides[0, n], sides[1, n] = both_sides(even, inner[NEAR + at], far[at])


def adjoint_step(step, now, later, back, flux, weights, added):
    top, bottom = edges()
    for row in range(step, EXT - step):
        vb, hb = back(1, row), back(2, row)
        au, av, ah = now[0, row], now[1, row], now[2, row]
        flux[0, row] = vb * au
        flux[1, row] = hb * ah + vb * av
        flux[2, row] = vb * ah + mix(av, weights)
    for row in range(step + 1, EXT - 1 - step):
        ub, hb = back(0, row), back(2, row)
        centre = [now[v, row] for v in range(VARS)]
        au, av, ah = centre
        across = [hb * ah + ub * au, ub * av, ub * ah + mix(au, weights)]
        turn = [0.98 * au - 0.03 * av, 0.98 * av + 0.03 * au, 0.98 * ah]
        for v in range(VARS):
            spread = 0.005 * centre[v]
            value = (
                turn[v]
                + (east(spread + across[v]) + west(spread - across[v]))
                + (0.005 * (now[v, row + 1] + now[v, row - 1]) + (flux[v, row + 1] - flux[v, row - 1]))
            )
            value = value + added(v, row)
            if row < HALO:
                value = value * top
            elif row >= HALO + STRIP:
                value = value * bottom
            later[v, row] = value


def fields_kernel(
    mult, variance, inc, got, expected, rep, sides, final0,
    report_out, fields, mult_out, model_out,
    raw, sems,
):
    copies = []
    for n, (source, target) in enumerate(
        ((mult, mult_out), (variance, raw.at[0]), (inc, raw.at[1]))
    ):
        copies.append(pltpu.make_async_copy(source, target, sems.at[n]))
        copies[n].start()
    chosen = jnp.where(owner_of_lane(), 1.0, 0.0).astype(f32).astype(bf16)
    spread = jnp.dot(
        jnp.concatenate(split(jnp.transpose(got[...])), axis=0),
        chosen,
        preferred_element_type=f32,
    )
    lanes = 4 * CAP * PARTS
    spread = spread[:lanes] + spread[lanes:]
    slot = lax.broadcasted_iota(jnp.int32, (PARTS, NX), 1) % CAP
    loads = []
    for g in range(4):
        value = jnp.zeros((PARTS, NX), f32)
        for i in range(CAP):
            at = (g * CAP + i) * PARTS
            value = jnp.where(slot == i, spread[at : at + PARTS], value)
        loads.append(value)
    for k in range(2):
        at = k * STEPS
        report_out[k] = expected[pl.ds(at, STEPS), :] + loads[3][at : at + STEPS]
    place = lax.broadcasted_iota(jnp.int32, (PARTS, NX), 0)
    first = lower_half()
    transposed = (((1,), (1,)), ((), ()))

    def field(report, load, j, rows):
        tiles = code_tiles(rows)
        count = 8 * len(tiles)
        windows = []
        for k in range(2):
            n = k * STEPS + j
            code, column = decode(report[0, n : n + 1])
            a, b = report[1, n : n + 1], report[2, n : n + 1]
            weight = load[n : n + 1]
            parts = []
            for share in ((1.0 - a) * weight, a * weight):
                own, following = (1.0 - b) * share, b * share
                block = []
                for t in tiles:
                    tile = jnp.where(code == place + (8 * t - LEVELS), following, 0.0)
                    block.append(jnp.where(code == place + 8 * t, own, tile))
                parts += list(split(jnp.concatenate(block, axis=0)))
            out = lax.dot_general(
                jnp.concatenate(parts, axis=0),
                one_hot_columns(column),
                transposed,
                preferred_element_type=f32,
            )
            total = out[:count] + out[count : 2 * count]
            total = total + west(out[2 * count : 3 * count] + out[3 * count :])
            windows.append(total)
        for at, t in enumerate(tiles):
            one, two = (w[8 * at : 8 * at + 8] for w in windows)
            v, r = t // (STRIP // 2), 2 * (t % (STRIP // 2))
            yield v, r, jnp.where(first, one, pltpu.roll(two, LEVELS, 0))
            yield v, r + 1, jnp.where(first, pltpu.roll(one, LEVELS, 0), two)

    for j in range(STEPS):
        base = FIRST_FIELD[j]
        for v, r, tile in field(rep, loads[1], j, list(range(STRIP))):
            fields[base + v * (STRIP + 2 * j) + j + r] = tile
        if j > 0:
            for v, r, tile in field(sides.at[0], loads[0], j, list(range(STRIP - j, STRIP))):
                if r >= STRIP - j:
                    fields[base + v * (STRIP + 2 * j) + j + r - STRIP] = tile
            for v, r, tile in field(sides.at[1], loads[2], j, list(range(j))):
                if r < j:
                    fields[base + v * (STRIP + 2 * j) + j + r + STRIP] = tile
    for copy in copies:
        copy.wait()
    for c in range(PARTS):
        model = raw[0, c] * mult_out[c] + raw[1, c]
        model_out[c] = model if c < LEVELS else model - final0[c - LEVELS]


def adjoint_kernel(
    mult, outer, mine, outermost, back, fields,
    image,
    state, flux,
):
    def backdrop(v, row):
        if v > 0 and row in (0, EXT - 1):
            return outermost[v - 1, 1 if row else 0]
        return back[v, row]

    first = lower_half()
    half = EXT // 2
    for v in range(VARS):
        for i in range(half):
            own, after = mine[v * half + i], outer[v * half + i]
            state[0, v, i] = -jnp.where(first, own, pltpu.roll(after, LEVELS, 0))
            state[0, v, i + half] = -jnp.where(first, pltpu.roll(own, LEVELS, 0), after)
    weights = mix_weights(SCALE * coupling.T)
    for step, j in enumerate(reversed(range(STEPS))):
        now, later = state.at[step % 2], state.at[(step + 1) % 2]

        def added(v, row):
            return fields[FIRST_FIELD[j] + v * (STRIP + 2 * j) + row - step - 1]

        adjoint_step(step, now, later, backdrop, flux, weights, added)
    last = STEPS % 2
    for v in range(VARS):
        image[:, v] = mult[:, v] + state_rows(state[last, v, HALO : HALO + STRIP])


def finish_kernel(
    image, report, model, incoming, image_out, report_out, model_out, first, sems
):
    copies = [
        pltpu.make_async_copy(image, image_out, sems.at[0]),
        pltpu.make_async_copy(model.at[LEVELS:], model_out.at[LEVELS:], sems.at[1]),
        pltpu.make_async_copy(report, report_out, sems.at[2]),
        pltpu.make_async_copy(first, model_out.at[:LEVELS], sems.at[3]),
    ]
    for copy in copies[:3]:
        copy.start()
    first[...] = model[:LEVELS] - incoming[...]
    copies[3].start()
    for copy in copies:
        copy.wait()


def vmem(count):
    return [pl.BlockSpec(memory_space=pltpu.VMEM)] * count


def hbm(count):
    return [pl.BlockSpec(memory_space=pltpu.HBM)] * count


def far_from_core(x):
    return pltpu.with_memory_space_constraint(x, pltpu.HBM)


def shaped(*shape, kind=f32):
    return jax.ShapeDtypeStruct(shape, kind)


def cost(kernel_us):
    return pl.CostEstimate(flops=int(kernel_us * 1e9), bytes_accessed=int(kernel_us * 3e6), transcendentals=0)


def per_device(
    multipliers,
    increments,
    background,
    error_variance,
    report_weights,
    report_variance,
    report_cells,
    report_offsets,
    report_counts,
):
    mult, inc, bg, variance = (
        x.reshape(PARTS, VARS, STRIP, NX)
        for x in (multipliers, increments, background, error_variance)
    )
    count = lax.axis_size("space")
    wins = lax.axis_size("win")
    tile = (PARTS, NX)
    rows = shaped(VARS, STRIP, *tile)
    extended = shaped(VARS, EXT, *tile)
    whole = shaped(PARTS, VARS, STRIP, NX)
    scratch = pltpu.VMEM(whole.shape, f32)
    near, inner, rep, inc_rows, bg_rows, mult_rows = pl.pallas_call(
        pack_kernel,
        name="pack",
        out_shape=(
            shaped(NEAR, *tile),
            shaped(NEAR + FAR, *tile),
            shaped(3, *tile),
            rows,
            rows,
            rows,
        ),
        in_specs=hbm(6),
        out_specs=vmem(6),
        scratch_shapes=[
            pltpu.VMEM((3, *whole.shape), f32),
            pltpu.VMEM(report_cells.shape, jnp.int32),
            pltpu.VMEM(report_offsets.shape, f32),
            pltpu.VMEM(report_counts.shape, jnp.int32),
            pltpu.SemaphoreType.DMA((6,)),
        ],
        compiler_params=params,
    )(
        *(
            far_from_core(x)
            for x in (inc, bg, mult, report_cells, report_offsets, report_counts)
        )
    )
    both = lambda pairs: pairs + [(target, source) for source, target in pairs]
    near = lax.ppermute(near, "space", both([(i, i + 1) for i in range(1, count - 1, 2)]))
    inner = lax.ppermute(inner, "space", both([(i, i + 1) for i in range(0, count, 2)]))
    hot = shaped(2 * STEPS, NX, NX, kind=bf16)
    far, along, rests, early = pl.pallas_call(
        prepare_kernel,
        name="prepare",
        out_shape=(shaped(FAR, *tile), hot, hot, shaped(*tile)),
        in_specs=vmem(4),
        out_specs=vmem(4),
        cost_estimate=cost(2),
        compiler_params=params,
    )(inc_rows, bg_rows, mult_rows, rep)
    far = lax.ppermute(far, "space", both([(i, i + 1) for i in range(1, count - 1, 2)]))
    final0, final1, send, expected, back = pl.pallas_call(
        tangent_kernel,
        name="tangent",
        out_shape=(
            shaped(LEVELS, VARS, STRIP, NX),
            shaped(LEVELS, VARS, STRIP, NX),
            shaped(OWNERS, 4 * CAP * PARTS),
            shaped(*tile),
            extended,
        ),
        in_specs=vmem(10),
        out_specs=vmem(2) + hbm(1) + vmem(2),
        scratch_shapes=[
            pltpu.VMEM((2, *extended.shape), f32),
            pltpu.VMEM((EXT, *tile), f32),
            pltpu.VMEM(tile, f32),
            pltpu.VMEM((OWNERS, 4 * CAP * PARTS), f32),
            pltpu.SemaphoreType.DMA,
        ],
        cost_estimate=cost(2),
        compiler_params=params,
    )(
        inc_rows, bg_rows, rep, along, rests, early, inner, near, report_weights, report_variance
    )
    got = lax.all_to_all(send, "space", split_axis=0, concat_axis=0, tiled=True)
    folded = shaped(VARS * EXT // 2, *tile)
    half = shaped(LEVELS, VARS, STRIP, NX)
    outer, final1, mine, outermost, sides = pl.pallas_call(
        outer_kernel,
        name="outer",
        out_shape=(
            folded, half, folded, shaped(2, 2, *tile), shaped(2, 3, *tile)
        ),
        in_specs=vmem(4),
        out_specs=vmem(5),
        cost_estimate=cost(OUTER_COST),
        compiler_params=params,
    )(mult_rows, inner, far, final1)
    incoming = lax.ppermute(final1, "win", [(i, i + 1) for i in range(wins - 1)])
    outer = lax.ppermute(outer, "win", [(i + 1, i) for i in range(wins - 1)])
    report, fields, mult_near, model = pl.pallas_call(
        fields_kernel,
        name="fields",
        out_shape=(
            shaped(2, STEPS, NX), shaped(FIRST_FIELD[STEPS], *tile), whole, whole
        ),
        in_specs=hbm(3) + vmem(5),
        out_specs=vmem(4),
        scratch_shapes=[pltpu.VMEM((2, *whole.shape), f32), pltpu.SemaphoreType.DMA((3,))],
        cost_estimate=cost(FIELDS_COST),
        compiler_params=params,
    )(
        *(far_from_core(x) for x in (mult, variance, inc)),
        got, expected, rep, sides, final0,
    )
    image = pl.pallas_call(
        adjoint_kernel,
        name="adjoint",
        out_shape=whole,
        in_specs=vmem(6),
        out_specs=vmem(1)[0],
        scratch_shapes=[
            pltpu.VMEM((2, *extended.shape), f32),
            pltpu.VMEM(extended.shape, f32),
        ],
        cost_estimate=cost(ADJOINT_COST),
        compiler_params=params,
    )(mult_near, outer, mine, outermost, back, fields)
    image, report, model = pl.pallas_call(
        finish_kernel,
        name="finish",
        out_shape=(whole, shaped(2, STEPS, NX), whole),
        in_specs=vmem(4),
        out_specs=hbm(3),
        scratch_shapes=[pltpu.VMEM(half.shape, f32), pltpu.SemaphoreType.DMA((4,))],
        compiler_params=params,
    )(image, report, model, incoming)
    return model.reshape(multipliers.shape), report, image.reshape(multipliers.shape)


def solution(mesh):
    state = P("win", None, "space", None)
    slots = P("win", None, "space")
    return jax.shard_map(
        per_device,
        mesh=mesh,
        in_specs=(state, state, state, state, slots, slots, slots, P("win", None, None, "space"), slots),
        out_specs=(state, slots, state),
        check_vma=False,
    )
```

```python
import jax
import jax.numpy as jnp
import numpy as np
from jax import lax
from jax.experimental import pallas as pl
from jax.experimental.pallas import tpu as pltpu
from jax.sharding import PartitionSpec as P

coupling = np.array(
    [[1.0, 0.55, 0.3, 0.15], [0.5, 0.9, 0.45, 0.25], [0.3, 0.4, 0.8, 0.35], [0.1, 0.2, 0.35, 0.7]],
    np.float32,
)
LEVELS = 4
VARS = 3
STEPS = 4
STRIP = 8
HALO = 4
EXT = STRIP + 2 * HALO
NX = 256
OWNERS = 64
CAP = 4
PARTS = 8
FIELD_TILES = VARS * HALO
NEAR = FIELD_TILES + VARS * (HALO - 1)
OUTER = FIELD_TILES
REPORTS = OUTER + 2
FAR = REPORTS + 3
CODES = VARS * STRIP * LEVELS
TILES = CODES // 8
FIRST_FIELD = [VARS * sum(STRIP + 2 * i for i in range(j)) for j in range(STEPS + 1)]
FIELDS_COST = 2
OUTER_COST = 0.01
ADJOINT_COST = 30
SCALE = 0.05
f32 = jnp.float32
bf16 = jnp.bfloat16
params = pltpu.CompilerParams(vmem_limit_bytes=20 * 2**20)


def east(z):
    return pltpu.roll(z, NX - 1, 1)


def west(z):
    return pltpu.roll(z, 1, 1)


def mix_weights(matrix):
    level = lax.broadcasted_iota(jnp.int32, (PARTS, NX), 0) % LEVELS
    weights = []
    for shift in range(1 - LEVELS, LEVELS):
        weight = jnp.zeros((PARTS, NX), f32)
        for l in range(LEVELS):
            if 0 <= l + shift < LEVELS:
                weight = jnp.where(level == l, float(matrix[l, l + shift]), weight)
        weights.append((shift, weight))
    return weights


def mix(z, weights):
    total = None
    for shift, weight in weights:
        term = weight * (z if shift == 0 else pltpu.roll(z, (-shift) % PARTS, 0))
        total = term if total is None else total + term
    return total


def split(x):
    high = x.astype(bf16)
    return high, (x - high.astype(f32)).astype(bf16)


def parity():
    return lax.axis_index("space") % 2 == 0


def state_rows(block):
    return jnp.swapaxes(block, 0, 1)


def owner_of_lane():
    lane = lax.broadcasted_iota(jnp.int32, (OWNERS, NX), 1)
    return lane // CAP == lax.broadcasted_iota(jnp.int32, (OWNERS, NX), 0)


def decode(report):
    p = report.astype(jnp.int32)
    channel = p >> 11
    level = (channel * 11) >> 5
    variable = channel - 3 * level
    code = (variable * STRIP + ((p >> 8) & 7)) * LEVELS + level
    return jnp.where(p < 0, -1024, code), p & (NX - 1)


def column_weights(report, n):
    _, column = decode(report[0, n : n + 1])
    share = report[1, n : n + 1]
    place = lax.broadcasted_iota(jnp.int32, (NX, NX), 0)
    following = jnp.where(place == ((column + 1) & (NX - 1)), share, 0.0)
    return split(jnp.where(place == column, 1.0 - share, following))


def one_hot_columns(column):
    place = lax.broadcasted_iota(jnp.int32, (NX, NX), 0)
    return jnp.where(place == column, 1.0, 0.0).astype(f32).astype(bf16)


def lower_half():
    return lax.broadcasted_iota(jnp.int32, (PARTS, NX), 0) < LEVELS


def code_tiles(rows):
    return [v * STRIP // 2 + t for v in range(VARS) for t in range(rows[0] // 2, rows[-1] // 2 + 1)]


def window_tiles(pair):
    first = lower_half()
    one = jnp.where(first, pair[0], pltpu.roll(pair[1], LEVELS, 0))
    two = jnp.where(first, pltpu.roll(pair[0], LEVELS, 0), pair[1])
    return one, two


def chosen_rows(low_end, rows, first, last):
    return jnp.where(low_end, rows[first:last], rows[STRIP - last : STRIP - first])


def near_halo(low_end, inc_rows, bg_rows, out):
    for v in range(VARS):
        at = v * HALO
        out[at : at + HALO] = chosen_rows(low_end, inc_rows[v], 0, HALO)
        at = FIELD_TILES + v * (HALO - 1)
        out[at : at + HALO - 1] = chosen_rows(low_end, bg_rows[v], 0, HALO - 1)


def far_halo(low_end, mult_rows, bg_rows, rep, out):
    for v in range(VARS):
        at = v * HALO
        out[at : at + HALO] = chosen_rows(low_end, mult_rows[v], 0, HALO)
        if v > 0:
            at = OUTER + v - 1
            out[at : at + 1] = chosen_rows(low_end, bg_rows[v], HALO - 1, HALO)
    out[REPORTS:] = rep[...]


def pack_kernel(
    inc, bg, mult, cells, offsets, counts,
    near, inner, rep, inc_rows, bg_rows, mult_rows,
    raw, raw_cells, raw_offsets, raw_counts, sems,
):
    copies = []
    for n, (source, target) in enumerate(
        (
            (inc, raw.at[0]),
            (bg, raw.at[1]),
            (mult, raw.at[2]),
            (cells, raw_cells),
            (offsets, raw_offsets),
            (counts, raw_counts),
        )
    ):
        copies.append(pltpu.make_async_copy(source, target, sems.at[n]))
        copies[n].start()
    even = parity()
    odd = jnp.logical_not(even)
    for f, rows_out in enumerate((inc_rows, bg_rows, mult_rows)):
        copies[f].wait()
        for v in range(VARS):
            rows_out[v] = state_rows(raw[f, :, v])
    near_halo(even, inc_rows, bg_rows, near)
    near_halo(odd, inc_rows, bg_rows, inner)
    for copy in copies[3:]:
        copy.wait()
    slot = lax.broadcasted_iota(jnp.int32, (PARTS, NX), 1) % CAP
    count = jnp.concatenate([raw_counts[0], raw_counts[1]], axis=0).astype(f32).astype(bf16)
    spread = jnp.where(owner_of_lane(), 1.0, 0.0).astype(f32).astype(bf16)
    live = slot.astype(f32) < jnp.dot(count, spread, preferred_element_type=f32)
    cell = jnp.concatenate([raw_cells[0], raw_cells[1]], axis=0).astype(f32)
    rep[0] = jnp.where(live, cell, -1.0)
    for k in range(2):
        for j in range(STEPS):
            for side in range(2):
                rep[1 + side, pl.ds(k * STEPS + j, 1), :] = raw_offsets[k, j, pl.ds(side, 1), :]
    far_halo(odd, mult_rows, bg_rows, rep, inner.at[NEAR:])


def sample(rows, j, rep, weights, rests, vals):
    pairs = [
        window_tiles((rows[v][r], rows[v][r + 1])) for v in range(VARS) for r in range(0, STRIP, 2)
    ]
    place = lax.broadcasted_iota(jnp.int32, (PARTS, NX), 0)
    for k in range(2):
        n = k * STEPS + j
        high, low = split(jnp.concatenate([pair[k] for pair in pairs], axis=0))
        code, _ = decode(rep[0, n : n + 1])
        picked = jnp.dot(
            jnp.concatenate([high, low], axis=0), weights[n], preferred_element_type=f32
        )
        rest = jnp.dot(high, rests[n], preferred_element_type=f32)
        sums = [jnp.zeros((PARTS, NX), f32) for _ in range(2)]
        for t in range(TILES):
            at = t * 8
            value = picked[at : at + 8] + (picked[CODES + at : CODES + at + 8] + rest[at : at + 8])
            sums = [
                jnp.where(code == place + at, value, sums[0]),
                jnp.where(code == place + (at - LEVELS), value, sums[1]),
            ]
        b = rep[2, n : n + 1]
        value = (1.0 - b) * sums[0] + b * sums[1]
        vals[pl.ds(n, 1), :] = jnp.sum(value, axis=0, keepdims=True)


def tangent_rows(get, back, raised, weights, rows, put):
    for row in sorted({near for row in rows for near in (row - 1, row, row + 1)}):
        raised[row] = mix(get(2, row), weights)
    for row in rows:
        ub, vb, hb = back(0, row), back(1, row), back(2, row)
        centre = [get(v, row) for v in range(VARS)]
        up = [get(v, row + 1) for v in range(VARS)]
        down = [get(v, row - 1) for v in range(VARS)]
        e = [east(z) for z in centre]
        w = [west(z) for z in centre]
        cols = [e[v] - w[v] for v in range(VARS)]
        slopes = [up[v] - down[v] for v in range(VARS)]
        smooth = [up[v] + down[v] + (e[v] + w[v]) for v in range(VARS)]
        lift = raised[row]
        push_c = east(lift) - west(lift)
        push_r = raised[row + 1] - raised[row - 1]
        new = [
            0.98 * centre[0]
            + 0.03 * centre[1]
            + 0.005 * smooth[0]
            - push_c
            - (ub * cols[0] + vb * slopes[0]),
            0.98 * centre[1]
            - 0.03 * centre[0]
            + 0.005 * smooth[1]
            - push_r
            - (ub * cols[1] + vb * slopes[1]),
            0.98 * centre[2]
            + 0.005 * smooth[2]
            - hb * (cols[0] + slopes[1])
            - (ub * cols[2] + vb * slopes[2]),
        ]
        for v in range(VARS):
            put(v, row, new[v])


def inside(step):
    return range(HALO + 1 + step, HALO + STRIP - 1 - step)


def prepare_kernel(
    inc_rows, bg_rows, mult_rows, rep, far, along, rests, vals, known, raised
):
    far_halo(parity(), mult_rows, bg_rows, rep, far)
    for n in range(2 * STEPS):
        along[n], rests[n] = column_weights(rep, n)
    vals[...] = jnp.zeros((PARTS, NX), f32)
    rows = [[inc_rows[v, r] for r in range(STRIP)] for v in range(VARS)]
    sample(rows, 0, rep, along, rests, vals)
    weights = mix_weights(SCALE * coupling)
    for step in range(STEPS - 1):
        before = inc_rows if step == 0 else known.at[step - 1]

        def put(v, row, value):
            known[step, v, row - HALO] = value

        tangent_rows(
            lambda v, row: before[v, row - HALO],
            lambda v, row: SCALE * bg_rows[v, row - HALO],
            raised,
            weights,
            inside(step),
            put,
        )


def edges():
    s = lax.axis_index("space")
    top = jnp.where(s > 0, 1.0, 0.0).astype(f32)
    bottom = jnp.where(s < OWNERS - 1, 1.0, 0.0).astype(f32)
    return top, bottom


def both_sides(even, a, b):
    return jnp.where(even, b, a), jnp.where(even, a, b)


def send_out(vals, owned, owned_variance, expected, send, packed, sem):
    own = jnp.concatenate([owned[0], owned[1]], axis=0)
    expected[...] = own * jnp.concatenate([owned_variance[0], owned_variance[1]], axis=0)
    slot = lax.broadcasted_iota(jnp.int32, (PARTS, NX), 1) % CAP
    pieces = []
    for piece in (pltpu.roll(own, CAP, 1), own, pltpu.roll(own, NX - CAP, 1), vals[...]):
        for i in range(CAP):
            pieces.append(jnp.where(slot == i, piece, 0.0))
    chosen = jnp.where(owner_of_lane(), 1.0, 0.0).astype(f32).astype(bf16)
    both = lax.dot_general(
        chosen,
        jnp.concatenate(split(jnp.concatenate(pieces, axis=0)), axis=0),
        (((1,), (1,)), ((), ())),
        preferred_element_type=f32,
    )
    lanes = 4 * CAP * PARTS
    packed[...] = both[:, :lanes] + both[:, lanes:]
    copy = pltpu.make_async_copy(packed, send, sem)
    copy.start()
    return copy


def tangent_kernel(
    inc_rows, bg_rows, rep, along, rests, early, known, got_a, got_near, owned, owned_variance,
    final0, final1, send, expected, back,
    state, raised, vals, packed, sem,
):
    even = parity()
    top, bottom = edges()
    end = HALO + STRIP
    for v in range(VARS):
        at = v * HALO
        low, high = both_sides(even, got_a[at : at + HALO], got_near[at : at + HALO])
        state[0, v, :HALO] = low
        state[0, v, end:] = high
        at = FIELD_TILES + v * (HALO - 1)
        low, high = both_sides(even, got_a[at : at + HALO - 1], got_near[at : at + HALO - 1])
        back[v, 1:HALO] = SCALE * low
        back[v, HALO:end] = SCALE * bg_rows[v]
        back[v, end : EXT - 1] = SCALE * high
        back[v, 0] = jnp.zeros((PARTS, NX), f32)
        back[v, EXT - 1] = jnp.zeros((PARTS, NX), f32)

    weights = mix_weights(SCALE * coupling)
    vals[...] = early[...]

    def get_at(j, v, row):
        if j == 0 and HALO <= row < end:
            return inc_rows[v, row - HALO]
        if j > 0 and row in inside(j - 1):
            return known[j - 1, v, row - HALO]
        return state[j, v, row]

    def advance(j, rows):
        def put(v, row, value):
            if row < HALO:
                value = value * top
            elif row >= end:
                value = value * bottom
            state[j + 1, v, row] = value

        tangent_rows(
            lambda v, row: get_at(j, v, row), lambda v, row: back[v, row], raised, weights, rows, put
        )

    for j in range(STEPS - 1):
        advance(j, [row for row in range(j + 2, EXT - 2 - j) if row not in inside(j)])
        rows = [[get_at(j + 1, v, HALO + r) for r in range(STRIP)] for v in range(VARS)]
        sample(rows, j + 1, rep, along, rests, vals)
    copy = send_out(vals, owned, owned_variance, expected, send, packed, sem)
    for j in range(STEPS - 1):
        advance(j, [j + 1, EXT - 2 - j])
    advance(STEPS - 1, list(range(HALO, end)))
    last = STEPS
    for v in range(VARS):
        value = state_rows(state[last, v, HALO : HALO + STRIP])
        final0[:, v] = value[:LEVELS]
        final1[:, v] = value[LEVELS:]
    copy.wait()


def outer_kernel(mult_rows, inner, far, final1, out, final_out, mine, outermost, sides):
    even = parity()
    half = EXT // 2
    final_out[...] = final1[...]
    for v in range(VARS):
        at = v * HALO
        low, high = both_sides(
            even, inner[NEAR + at : NEAR + at + HALO], far[at : at + HALO]
        )
        rows = (
            [low[i] for i in range(HALO)]
            + [mult_rows[v, r] for r in range(STRIP)]
            + [high[i] for i in range(HALO)]
        )
        for i in range(half):
            n = v * half + i
            out[n], mine[n] = window_tiles((rows[i], rows[i + half]))
    for v in (1, 2):
        at = OUTER + v - 1
        low, high = both_sides(even, inner[NEAR + at], far[at])
        outermost[v - 1, 0], outermost[v - 1, 1] = SCALE * low, SCALE * high
    for n in range(3):
        at = REPORTS + n
        sides[0, n], sides[1, n] = both_sides(even, inner[NEAR + at], far[at])


def adjoint_step(step, now, later, back, flux, weights, added):
    top, bottom = edges()
    for row in range(step, EXT - step):
        vb, hb = back(1, row), back(2, row)
        au, av, ah = now[0, row], now[1, row], now[2, row]
        flux[0, row] = vb * au
        flux[1, row] = hb * ah + vb * av
        flux[2, row] = vb * ah + mix(av, weights)
    for row in range(step + 1, EXT - 1 - step):
        ub, hb = back(0, row), back(2, row)
        centre = [now[v, row] for v in range(VARS)]
        au, av, ah = centre
        across = [hb * ah + ub * au, ub * av, ub * ah + mix(au, weights)]
        turn = [0.98 * au - 0.03 * av, 0.98 * av + 0.03 * au, 0.98 * ah]
        for v in range(VARS):
            spread = 0.005 * centre[v]
            value = (
                turn[v]
                + (east(spread + across[v]) + west(spread - across[v]))
                + (0.005 * (now[v, row + 1] + now[v, row - 1]) + (flux[v, row + 1] - flux[v, row - 1]))
            )
            value = value + added(v, row)
            if row < HALO:
                value = value * top
            elif row >= HALO + STRIP:
                value = value * bottom
            later[v, row] = value


def fields_kernel(
    mult, variance, inc, got, expected, rep, sides, final0,
    report_out, fields, mult_out, model_out,
    raw, sems,
):
    copies = []
    for n, (source, target) in enumerate(
        ((mult, mult_out), (variance, raw.at[0]), (inc, raw.at[1]))
    ):
        copies.append(pltpu.make_async_copy(source, target, sems.at[n]))
        copies[n].start()
    chosen = jnp.where(owner_of_lane(), 1.0, 0.0).astype(f32).astype(bf16)
    spread = jnp.dot(
        jnp.concatenate(split(jnp.transpose(got[...])), axis=0),
        chosen,
        preferred_element_type=f32,
    )
    lanes = 4 * CAP * PARTS
    spread = spread[:lanes] + spread[lanes:]
    slot = lax.broadcasted_iota(jnp.int32, (PARTS, NX), 1) % CAP
    loads = []
    for g in range(4):
        value = jnp.zeros((PARTS, NX), f32)
        for i in range(CAP):
            at = (g * CAP + i) * PARTS
            value = jnp.where(slot == i, spread[at : at + PARTS], value)
        loads.append(value)
    for k in range(2):
        at = k * STEPS
        report_out[k] = expected[pl.ds(at, STEPS), :] + loads[3][at : at + STEPS]
    place = lax.broadcasted_iota(jnp.int32, (PARTS, NX), 0)
    first = lower_half()
    transposed = (((1,), (1,)), ((), ()))

    def field(report, load, j, rows):
        tiles = code_tiles(rows)
        count = 8 * len(tiles)
        windows = []
        for k in range(2):
            n = k * STEPS + j
            code, column = decode(report[0, n : n + 1])
            a, b = report[1, n : n + 1], report[2, n : n + 1]
            weight = load[n : n + 1]
            parts = []
            for share in ((1.0 - a) * weight, a * weight):
                own, following = (1.0 - b) * share, b * share
                block = []
                for t in tiles:
                    tile = jnp.where(code == place + (8 * t - LEVELS), following, 0.0)
                    block.append(jnp.where(code == place + 8 * t, own, tile))
                parts += list(split(jnp.concatenate(block, axis=0)))
            out = lax.dot_general(
                jnp.concatenate(parts, axis=0),
                one_hot_columns(column),
                transposed,
                preferred_element_type=f32,
            )
            total = out[:count] + out[count : 2 * count]
            total = total + west(out[2 * count : 3 * count] + out[3 * count :])
            windows.append(total)
        for at, t in enumerate(tiles):
            one, two = (w[8 * at : 8 * at + 8] for w in windows)
            v, r = t // (STRIP // 2), 2 * (t % (STRIP // 2))
            yield v, r, jnp.where(first, one, pltpu.roll(two, LEVELS, 0))
            yield v, r + 1, jnp.where(first, pltpu.roll(one, LEVELS, 0), two)

    for j in range(STEPS):
        base = FIRST_FIELD[j]
        for v, r, tile in field(rep, loads[1], j, list(range(STRIP))):
            fields[base + v * (STRIP + 2 * j) + j + r] = tile
        if j > 0:
            for v, r, tile in field(sides.at[0], loads[0], j, list(range(STRIP - j, STRIP))):
                if r >= STRIP - j:
                    fields[base + v * (STRIP + 2 * j) + j + r - STRIP] = tile
            for v, r, tile in field(sides.at[1], loads[2], j, list(range(j))):
                if r < j:
                    fields[base + v * (STRIP + 2 * j) + j + r + STRIP] = tile
    for copy in copies:
        copy.wait()
    for c in range(PARTS):
        model = raw[0, c] * mult_out[c] + raw[1, c]
        model_out[c] = model if c < LEVELS else model - final0[c - LEVELS]


def adjoint_kernel(
    mult, outer, mine, outermost, back, fields,
    image,
    state, flux,
):
    def backdrop(v, row):
        if v > 0 and row in (0, EXT - 1):
            return outermost[v - 1, 1 if row else 0]
        return back[v, row]

    first = lower_half()
    half = EXT // 2
    for v in range(VARS):
        for i in range(half):
            own, after = mine[v * half + i], outer[v * half + i]
            state[0, v, i] = -jnp.where(first, own, pltpu.roll(after, LEVELS, 0))
            state[0, v, i + half] = -jnp.where(first, pltpu.roll(own, LEVELS, 0), after)
    weights = mix_weights(SCALE * coupling.T)
    for step, j in enumerate(reversed(range(STEPS))):
        now, later = state.at[step % 2], state.at[(step + 1) % 2]

        def added(v, row):
            return fields[FIRST_FIELD[j] + v * (STRIP + 2 * j) + row - step - 1]

        adjoint_step(step, now, later, backdrop, flux, weights, added)
    last = STEPS % 2
    for v in range(VARS):
        image[:, v] = mult[:, v] + state_rows(state[last, v, HALO : HALO + STRIP])


def finish_kernel(
    image, report, model, incoming, image_out, report_out, model_out, first, sems
):
    copies = [
        pltpu.make_async_copy(image, image_out, sems.at[0]),
        pltpu.make_async_copy(model.at[LEVELS:], model_out.at[LEVELS:], sems.at[1]),
        pltpu.make_async_copy(report, report_out, sems.at[2]),
        pltpu.make_async_copy(first, model_out.at[:LEVELS], sems.at[3]),
    ]
    for copy in copies[:3]:
        copy.start()
    first[...] = model[:LEVELS] - incoming[...]
    copies[3].start()
    for copy in copies:
        copy.wait()


def vmem(count):
    return [pl.BlockSpec(memory_space=pltpu.VMEM)] * count


def hbm(count):
    return [pl.BlockSpec(memory_space=pltpu.HBM)] * count


def far_from_core(x):
    return pltpu.with_memory_space_constraint(x, pltpu.HBM)


def shaped(*shape, kind=f32):
    return jax.ShapeDtypeStruct(shape, kind)


def cost(kernel_us):
    return pl.CostEstimate(flops=int(kernel_us * 1e9), bytes_accessed=int(kernel_us * 3e6), transcendentals=0)


def per_device(
    multipliers,
    increments,
    background,
    error_variance,
    report_weights,
    report_variance,
    report_cells,
    report_offsets,
    report_counts,
):
    mult, inc, bg, variance = (
        x.reshape(PARTS, VARS, STRIP, NX)
        for x in (multipliers, increments, background, error_variance)
    )
    count = lax.axis_size("space")
    wins = lax.axis_size("win")
    tile = (PARTS, NX)
    rows = shaped(VARS, STRIP, *tile)
    extended = shaped(VARS, EXT, *tile)
    whole = shaped(PARTS, VARS, STRIP, NX)
    scratch = pltpu.VMEM(whole.shape, f32)
    near, inner, rep, inc_rows, bg_rows, mult_rows = pl.pallas_call(
        pack_kernel,
        name="pack",
        out_shape=(
            shaped(NEAR, *tile),
            shaped(NEAR + FAR, *tile),
            shaped(3, *tile),
            rows,
            rows,
            rows,
        ),
        in_specs=hbm(6),
        out_specs=vmem(6),
        scratch_shapes=[
            pltpu.VMEM((3, *whole.shape), f32),
            pltpu.VMEM(report_cells.shape, jnp.int32),
            pltpu.VMEM(report_offsets.shape, f32),
            pltpu.VMEM(report_counts.shape, jnp.int32),
            pltpu.SemaphoreType.DMA((6,)),
        ],
        compiler_params=params,
    )(
        *(
            far_from_core(x)
            for x in (inc, bg, mult, report_cells, report_offsets, report_counts)
        )
    )
    both = lambda pairs: pairs + [(target, source) for source, target in pairs]
    near = lax.ppermute(near, "space", both([(i, i + 1) for i in range(1, count - 1, 2)]))
    inner = lax.ppermute(inner, "space", both([(i, i + 1) for i in range(0, count, 2)]))
    hot = shaped(2 * STEPS, NX, NX, kind=bf16)
    far, along, rests, early, known = pl.pallas_call(
        prepare_kernel,
        name="prepare",
        out_shape=(
            shaped(FAR, *tile), hot, hot, shaped(*tile), shaped(STEPS - 1, VARS, STRIP, *tile)
        ),
        in_specs=vmem(4),
        out_specs=vmem(5),
        scratch_shapes=[pltpu.VMEM((EXT, *tile), f32)],
        cost_estimate=cost(2),
        compiler_params=params,
    )(inc_rows, bg_rows, mult_rows, rep)
    far = lax.ppermute(far, "space", both([(i, i + 1) for i in range(1, count - 1, 2)]))
    final0, final1, send, expected, back = pl.pallas_call(
        tangent_kernel,
        name="tangent",
        out_shape=(
            shaped(LEVELS, VARS, STRIP, NX),
            shaped(LEVELS, VARS, STRIP, NX),
            shaped(OWNERS, 4 * CAP * PARTS),
            shaped(*tile),
            extended,
        ),
        in_specs=vmem(11),
        out_specs=vmem(2) + hbm(1) + vmem(2),
        scratch_shapes=[
            pltpu.VMEM((STEPS + 1, *extended.shape), f32),
            pltpu.VMEM((EXT, *tile), f32),
            pltpu.VMEM(tile, f32),
            pltpu.VMEM((OWNERS, 4 * CAP * PARTS), f32),
            pltpu.SemaphoreType.DMA,
        ],
        cost_estimate=cost(2),
        compiler_params=params,
    )(
        inc_rows, bg_rows, rep, along, rests, early, known, inner, near, report_weights,
        report_variance,
    )
    got = lax.all_to_all(send, "space", split_axis=0, concat_axis=0, tiled=True)
    folded = shaped(VARS * EXT // 2, *tile)
    half = shaped(LEVELS, VARS, STRIP, NX)
    outer, final1, mine, outermost, sides = pl.pallas_call(
        outer_kernel,
        name="outer",
        out_shape=(
            folded, half, folded, shaped(2, 2, *tile), shaped(2, 3, *tile)
        ),
        in_specs=vmem(4),
        out_specs=vmem(5),
        cost_estimate=cost(OUTER_COST),
        compiler_params=params,
    )(mult_rows, inner, far, final1)
    incoming = lax.ppermute(final1, "win", [(i, i + 1) for i in range(wins - 1)])
    outer = lax.ppermute(outer, "win", [(i + 1, i) for i in range(wins - 1)])
    report, fields, mult_near, model = pl.pallas_call(
        fields_kernel,
        name="fields",
        out_shape=(
            shaped(2, STEPS, NX), shaped(FIRST_FIELD[STEPS], *tile), whole, whole
        ),
        in_specs=hbm(3) + vmem(5),
        out_specs=vmem(4),
        scratch_shapes=[pltpu.VMEM((2, *whole.shape), f32), pltpu.SemaphoreType.DMA((3,))],
        cost_estimate=cost(FIELDS_COST),
        compiler_params=params,
    )(
        *(far_from_core(x) for x in (mult, variance, inc)),
        got, expected, rep, sides, final0,
    )
    image = pl.pallas_call(
        adjoint_kernel,
        name="adjoint",
        out_shape=whole,
        in_specs=vmem(6),
        out_specs=vmem(1)[0],
        scratch_shapes=[
            pltpu.VMEM((2, *extended.shape), f32),
            pltpu.VMEM(extended.shape, f32),
        ],
        cost_estimate=cost(ADJOINT_COST),
        compiler_params=params,
    )(mult_near, outer, mine, outermost, back, fields)
    image, report, model = pl.pallas_call(
        finish_kernel,
        name="finish",
        out_shape=(whole, shaped(2, STEPS, NX), whole),
        in_specs=vmem(4),
        out_specs=hbm(3),
        scratch_shapes=[pltpu.VMEM(half.shape, f32), pltpu.SemaphoreType.DMA((4,))],
        compiler_params=params,
    )(image, report, model, incoming)
    return model.reshape(multipliers.shape), report, image.reshape(multipliers.shape)


def solution(mesh):
    state = P("win", None, "space", None)
    slots = P("win", None, "space")
    return jax.shard_map(
        per_device,
        mesh=mesh,
        in_specs=(state, state, state, state, slots, slots, slots, P("win", None, None, "space"), slots),
        out_specs=(state, slots, state),
        check_vma=False,
    )
```

```python
import jax
import jax.numpy as jnp
import numpy as np
from jax import lax
from jax.experimental import pallas as pl
from jax.experimental.pallas import tpu as pltpu
from jax.sharding import PartitionSpec as P

coupling = np.array(
    [[1.0, 0.55, 0.3, 0.15], [0.5, 0.9, 0.45, 0.25], [0.3, 0.4, 0.8, 0.35], [0.1, 0.2, 0.35, 0.7]],
    np.float32,
)
LEVELS = 4
VARS = 3
STEPS = 4
STRIP = 8
HALO = 4
EXT = STRIP + 2 * HALO
NX = 256
OWNERS = 64
CAP = 4
PARTS = 8
FIELD_TILES = VARS * HALO
NEAR = FIELD_TILES + VARS * (HALO - 1)
OUTER = FIELD_TILES
REPORTS = OUTER + 2
FAR = REPORTS + 3
CODES = VARS * STRIP * LEVELS
TILES = CODES // 8
FIRST_FIELD = [VARS * sum(STRIP + 2 * i for i in range(j)) for j in range(STEPS + 1)]
FIELDS_COST = 2
OUTER_COST = 0.01
ADJOINT_COST = 30
SCALE = 0.05
f32 = jnp.float32
bf16 = jnp.bfloat16
params = pltpu.CompilerParams(vmem_limit_bytes=20 * 2**20)


def east(z):
    return pltpu.roll(z, NX - 1, 1)


def west(z):
    return pltpu.roll(z, 1, 1)


def mix_weights(matrix):
    level = lax.broadcasted_iota(jnp.int32, (PARTS, NX), 0) % LEVELS
    weights = []
    for shift in range(1 - LEVELS, LEVELS):
        weight = jnp.zeros((PARTS, NX), f32)
        for l in range(LEVELS):
            if 0 <= l + shift < LEVELS:
                weight = jnp.where(level == l, float(matrix[l, l + shift]), weight)
        weights.append((shift, weight))
    return weights


def mix(z, weights):
    total = None
    for shift, weight in weights:
        term = weight * (z if shift == 0 else pltpu.roll(z, (-shift) % PARTS, 0))
        total = term if total is None else total + term
    return total


def split(x):
    high = x.astype(bf16)
    return high, (x - high.astype(f32)).astype(bf16)


def parity():
    return lax.axis_index("space") % 2 == 0


def state_rows(block):
    return jnp.swapaxes(block, 0, 1)


def owner_of_lane():
    lane = lax.broadcasted_iota(jnp.int32, (OWNERS, NX), 1)
    return lane // CAP == lax.broadcasted_iota(jnp.int32, (OWNERS, NX), 0)


def decode(report):
    p = report.astype(jnp.int32)
    channel = p >> 11
    level = (channel * 11) >> 5
    variable = channel - 3 * level
    code = (variable * STRIP + ((p >> 8) & 7)) * LEVELS + level
    return jnp.where(p < 0, -1024, code), p & (NX - 1)


def column_weights(report, n):
    _, column = decode(report[0, n : n + 1])
    share = report[1, n : n + 1]
    place = lax.broadcasted_iota(jnp.int32, (NX, NX), 0)
    following = jnp.where(place == ((column + 1) & (NX - 1)), share, 0.0)
    return split(jnp.where(place == column, 1.0 - share, following))


def one_hot_columns(column):
    place = lax.broadcasted_iota(jnp.int32, (NX, NX), 0)
    return jnp.where(place == column, 1.0, 0.0).astype(f32).astype(bf16)


def lower_half():
    return lax.broadcasted_iota(jnp.int32, (PARTS, NX), 0) < LEVELS


def code_tiles(rows):
    return [v * STRIP // 2 + t for v in range(VARS) for t in range(rows[0] // 2, rows[-1] // 2 + 1)]


def window_tiles(pair):
    first = lower_half()
    one = jnp.where(first, pair[0], pltpu.roll(pair[1], LEVELS, 0))
    two = jnp.where(first, pltpu.roll(pair[0], LEVELS, 0), pair[1])
    return one, two


def chosen_rows(low_end, rows, first, last):
    return jnp.where(low_end, rows[first:last], rows[STRIP - last : STRIP - first])


def near_halo(low_end, inc_rows, bg_rows, out):
    for v in range(VARS):
        at = v * HALO
        out[at : at + HALO] = chosen_rows(low_end, inc_rows[v], 0, HALO)
        at = FIELD_TILES + v * (HALO - 1)
        out[at : at + HALO - 1] = chosen_rows(low_end, bg_rows[v], 0, HALO - 1)


def far_halo(low_end, mult_rows, bg_rows, rep, out):
    for v in range(VARS):
        at = v * HALO
        out[at : at + HALO] = chosen_rows(low_end, mult_rows[v], 0, HALO)
        if v > 0:
            at = OUTER + v - 1
            out[at : at + 1] = chosen_rows(low_end, bg_rows[v], HALO - 1, HALO)
    out[REPORTS:] = rep[...]


def pack_kernel(
    inc, bg, mult, cells, offsets, counts,
    near, inner, rep, inc_rows, bg_rows, mult_rows,
    raw, raw_cells, raw_offsets, raw_counts, sems,
):
    copies = []
    for n, (source, target) in enumerate(
        (
            (inc, raw.at[0]),
            (bg, raw.at[1]),
            (mult, raw.at[2]),
            (cells, raw_cells),
            (offsets, raw_offsets),
            (counts, raw_counts),
        )
    ):
        copies.append(pltpu.make_async_copy(source, target, sems.at[n]))
        copies[n].start()
    even = parity()
    odd = jnp.logical_not(even)
    for f, rows_out in enumerate((inc_rows, bg_rows, mult_rows)):
        copies[f].wait()
        for v in range(VARS):
            rows_out[v] = state_rows(raw[f, :, v])
    near_halo(even, inc_rows, bg_rows, near)
    near_halo(odd, inc_rows, bg_rows, inner)
    for copy in copies[3:]:
        copy.wait()
    slot = lax.broadcasted_iota(jnp.int32, (PARTS, NX), 1) % CAP
    count = jnp.concatenate([raw_counts[0], raw_counts[1]], axis=0).astype(f32).astype(bf16)
    spread = jnp.where(owner_of_lane(), 1.0, 0.0).astype(f32).astype(bf16)
    live = slot.astype(f32) < jnp.dot(count, spread, preferred_element_type=f32)
    cell = jnp.concatenate([raw_cells[0], raw_cells[1]], axis=0).astype(f32)
    rep[0] = jnp.where(live, cell, -1.0)
    for k in range(2):
        for j in range(STEPS):
            for side in range(2):
                rep[1 + side, pl.ds(k * STEPS + j, 1), :] = raw_offsets[k, j, pl.ds(side, 1), :]
    far_halo(odd, mult_rows, bg_rows, rep, inner.at[NEAR:])


def sample(rows, j, rep, weights, rests, vals):
    pairs = [
        window_tiles((rows[v][r], rows[v][r + 1])) for v in range(VARS) for r in range(0, STRIP, 2)
    ]
    place = lax.broadcasted_iota(jnp.int32, (PARTS, NX), 0)
    for k in range(2):
        n = k * STEPS + j
        high, low = split(jnp.concatenate([pair[k] for pair in pairs], axis=0))
        code, _ = decode(rep[0, n : n + 1])
        picked = jnp.dot(
            jnp.concatenate([high, low], axis=0), weights[n], preferred_element_type=f32
        )
        rest = jnp.dot(high, rests[n], preferred_element_type=f32)
        sums = [jnp.zeros((PARTS, NX), f32) for _ in range(2)]
        for t in range(TILES):
            at = t * 8
            value = picked[at : at + 8] + (picked[CODES + at : CODES + at + 8] + rest[at : at + 8])
            sums = [
                jnp.where(code == place + at, value, sums[0]),
                jnp.where(code == place + (at - LEVELS), value, sums[1]),
            ]
        b = rep[2, n : n + 1]
        value = (1.0 - b) * sums[0] + b * sums[1]
        vals[pl.ds(n, 1), :] = jnp.sum(value, axis=0, keepdims=True)


def tangent_rows(get, back, raised, weights, rows, put):
    for row in sorted({near for row in rows for near in (row - 1, row, row + 1)}):
        raised[row] = mix(get(2, row), weights)
    for row in rows:
        ub, vb, hb = back(0, row), back(1, row), back(2, row)
        centre = [get(v, row) for v in range(VARS)]
        up = [get(v, row + 1) for v in range(VARS)]
        down = [get(v, row - 1) for v in range(VARS)]
        e = [east(z) for z in centre]
        w = [west(z) for z in centre]
        cols = [e[v] - w[v] for v in range(VARS)]
        slopes = [up[v] - down[v] for v in range(VARS)]
        smooth = [up[v] + down[v] + (e[v] + w[v]) for v in range(VARS)]
        lift = raised[row]
        push_c = east(lift) - west(lift)
        push_r = raised[row + 1] - raised[row - 1]
        new = [
            0.98 * centre[0]
            + 0.03 * centre[1]
            + 0.005 * smooth[0]
            - push_c
            - (ub * cols[0] + vb * slopes[0]),
            0.98 * centre[1]
            - 0.03 * centre[0]
            + 0.005 * smooth[1]
            - push_r
            - (ub * cols[1] + vb * slopes[1]),
            0.98 * centre[2]
            + 0.005 * smooth[2]
            - hb * (cols[0] + slopes[1])
            - (ub * cols[2] + vb * slopes[2]),
        ]
        for v in range(VARS):
            put(v, row, new[v])


def inside(step):
    return range(HALO + 1 + step, HALO + STRIP - 1 - step)


def prepare_kernel(
    inc_rows, bg_rows, mult_rows, rep, far, along, rests, vals, known, raised
):
    far_halo(parity(), mult_rows, bg_rows, rep, far)
    for n in range(2 * STEPS):
        along[n], rests[n] = column_weights(rep, n)
    vals[...] = jnp.zeros((PARTS, NX), f32)
    rows = [[inc_rows[v, r] for r in range(STRIP)] for v in range(VARS)]
    sample(rows, 0, rep, along, rests, vals)
    weights = mix_weights(SCALE * coupling)
    for step in range(STEPS - 1):
        before = inc_rows if step == 0 else known.at[step - 1]

        def put(v, row, value):
            known[step, v, row - HALO] = value

        tangent_rows(
            lambda v, row: before[v, row - HALO],
            lambda v, row: SCALE * bg_rows[v, row - HALO],
            raised,
            weights,
            inside(step),
            put,
        )


def edges():
    s = lax.axis_index("space")
    top = jnp.where(s > 0, 1.0, 0.0).astype(f32)
    bottom = jnp.where(s < OWNERS - 1, 1.0, 0.0).astype(f32)
    return top, bottom


def both_sides(even, a, b):
    return jnp.where(even, b, a), jnp.where(even, a, b)


def send_out(vals, owned, owned_variance, expected, send, packed, sem):
    own = jnp.concatenate([owned[0], owned[1]], axis=0)
    expected[...] = own * jnp.concatenate([owned_variance[0], owned_variance[1]], axis=0)
    slot = lax.broadcasted_iota(jnp.int32, (PARTS, NX), 1) % CAP
    pieces = []
    for piece in (pltpu.roll(own, CAP, 1), own, pltpu.roll(own, NX - CAP, 1), vals[...]):
        for i in range(CAP):
            pieces.append(jnp.where(slot == i, piece, 0.0))
    chosen = jnp.where(owner_of_lane(), 1.0, 0.0).astype(f32).astype(bf16)
    both = lax.dot_general(
        chosen,
        jnp.concatenate(split(jnp.concatenate(pieces, axis=0)), axis=0),
        (((1,), (1,)), ((), ())),
        preferred_element_type=f32,
    )
    lanes = 4 * CAP * PARTS
    packed[...] = both[:, :lanes] + both[:, lanes:]
    copy = pltpu.make_async_copy(packed, send, sem)
    copy.start()
    return copy


def tangent_kernel(
    inc_rows, bg_rows, rep, along, rests, early, known, got_a, got_near, owned, owned_variance,
    final0, final1, send, expected, back,
    state, raised, vals, packed, sem,
):
    even = parity()
    top, bottom = edges()
    end = HALO + STRIP
    for v in range(VARS):
        at = v * HALO
        low, high = both_sides(even, got_a[at : at + HALO], got_near[at : at + HALO])
        state[0, v, :HALO] = low
        state[0, v, end:] = high
        at = FIELD_TILES + v * (HALO - 1)
        low, high = both_sides(even, got_a[at : at + HALO - 1], got_near[at : at + HALO - 1])
        back[v, 1:HALO] = SCALE * low
        back[v, HALO:end] = SCALE * bg_rows[v]
        back[v, end : EXT - 1] = SCALE * high
        back[v, 0] = jnp.zeros((PARTS, NX), f32)
        back[v, EXT - 1] = jnp.zeros((PARTS, NX), f32)

    weights = mix_weights(SCALE * coupling)
    vals[...] = early[...]

    def get_at(j, v, row):
        if j == 0 and HALO <= row < end:
            return inc_rows[v, row - HALO]
        if j > 0 and row in inside(j - 1):
            return known[j - 1, v, row - HALO]
        return state[j, v, row]

    def advance(j, rows):
        def put(v, row, value):
            if row < HALO:
                value = value * top
            elif row >= end:
                value = value * bottom
            state[j + 1, v, row] = value

        tangent_rows(
            lambda v, row: get_at(j, v, row), lambda v, row: back[v, row], raised, weights, rows, put
        )

    for j in range(STEPS - 1):
        advance(j, [row for row in range(j + 2, EXT - 2 - j) if row not in inside(j)])
        rows = [[get_at(j + 1, v, HALO + r) for r in range(STRIP)] for v in range(VARS)]
        sample(rows, j + 1, rep, along, rests, vals)
    copy = send_out(vals, owned, owned_variance, expected, send, packed, sem)
    @pl.when(lax.axis_index("space") >= 0)
    def while_it_leaves():
        for j in range(STEPS - 1):
            advance(j, [j + 1, EXT - 2 - j])
        advance(STEPS - 1, list(range(HALO, end)))
        last = STEPS
        for v in range(VARS):
            value = state_rows(state[last, v, HALO : HALO + STRIP])
            final0[:, v] = value[:LEVELS]
            final1[:, v] = value[LEVELS:]

    copy.wait()


def outer_kernel(mult_rows, inner, far, final1, out, final_out, mine, outermost, sides):
    even = parity()
    half = EXT // 2
    final_out[...] = final1[...]
    for v in range(VARS):
        at = v * HALO
        low, high = both_sides(
            even, inner[NEAR + at : NEAR + at + HALO], far[at : at + HALO]
        )
        rows = (
            [low[i] for i in range(HALO)]
            + [mult_rows[v, r] for r in range(STRIP)]
            + [high[i] for i in range(HALO)]
        )
        for i in range(half):
            n = v * half + i
            out[n], mine[n] = window_tiles((rows[i], rows[i + half]))
    for v in (1, 2):
        at = OUTER + v - 1
        low, high = both_sides(even, inner[NEAR + at], far[at])
        outermost[v - 1, 0], outermost[v - 1, 1] = SCALE * low, SCALE * high
    for n in range(3):
        at = REPORTS + n
        sides[0, n], sides[1, n] = both_sides(even, inner[NEAR + at], far[at])


def adjoint_step(step, now, later, back, flux, weights, added):
    top, bottom = edges()
    for row in range(step, EXT - step):
        vb, hb = back(1, row), back(2, row)
        au, av, ah = now[0, row], now[1, row], now[2, row]
        flux[0, row] = vb * au
        flux[1, row] = hb * ah + vb * av
        flux[2, row] = vb * ah
    for row in range(step + 1, EXT - 1 - step):
        ub, hb = back(0, row), back(2, row)
        centre = [now[v, row] for v in range(VARS)]
        au, av, ah = centre
        across = [hb * ah + ub * au, ub * av, ub * ah]
        lift = mix((east(au) - west(au)) + (now[1, row + 1] - now[1, row - 1]), weights)
        turn = [0.98 * au - 0.03 * av, 0.98 * av + 0.03 * au, 0.98 * ah + lift]
        for v in range(VARS):
            spread = 0.005 * centre[v]
            value = (
                turn[v]
                + (east(spread + across[v]) + west(spread - across[v]))
                + (0.005 * (now[v, row + 1] + now[v, row - 1]) + (flux[v, row + 1] - flux[v, row - 1]))
            )
            value = value + added(v, row)
            if row < HALO:
                value = value * top
            elif row >= HALO + STRIP:
                value = value * bottom
            later[v, row] = value


def fields_kernel(
    mult, variance, inc, got, expected, rep, sides, final0,
    report_out, fields, mult_out, model_out,
    raw, sems,
):
    copies = []
    for n, (source, target) in enumerate(
        ((mult, mult_out), (variance, raw.at[0]), (inc, raw.at[1]))
    ):
        copies.append(pltpu.make_async_copy(source, target, sems.at[n]))
        copies[n].start()
    chosen = jnp.where(owner_of_lane(), 1.0, 0.0).astype(f32).astype(bf16)
    spread = jnp.dot(
        jnp.concatenate(split(jnp.transpose(got[...])), axis=0),
        chosen,
        preferred_element_type=f32,
    )
    lanes = 4 * CAP * PARTS
    spread = spread[:lanes] + spread[lanes:]
    slot = lax.broadcasted_iota(jnp.int32, (PARTS, NX), 1) % CAP
    loads = []
    for g in range(4):
        value = jnp.zeros((PARTS, NX), f32)
        for i in range(CAP):
            at = (g * CAP + i) * PARTS
            value = jnp.where(slot == i, spread[at : at + PARTS], value)
        loads.append(value)
    for k in range(2):
        at = k * STEPS
        report_out[k] = expected[pl.ds(at, STEPS), :] + loads[3][at : at + STEPS]
    place = lax.broadcasted_iota(jnp.int32, (PARTS, NX), 0)
    first = lower_half()
    transposed = (((1,), (1,)), ((), ()))

    def field(report, load, j, rows):
        tiles = code_tiles(rows)
        count = 8 * len(tiles)
        windows = []
        for k in range(2):
            n = k * STEPS + j
            code, column = decode(report[0, n : n + 1])
            a, b = report[1, n : n + 1], report[2, n : n + 1]
            weight = load[n : n + 1]
            parts = []
            for share in ((1.0 - a) * weight, a * weight):
                own, following = (1.0 - b) * share, b * share
                block = []
                for t in tiles:
                    tile = jnp.where(code == place + (8 * t - LEVELS), following, 0.0)
                    block.append(jnp.where(code == place + 8 * t, own, tile))
                parts += list(split(jnp.concatenate(block, axis=0)))
            out = lax.dot_general(
                jnp.concatenate(parts, axis=0),
                one_hot_columns(column),
                transposed,
                preferred_element_type=f32,
            )
            total = out[:count] + out[count : 2 * count]
            total = total + west(out[2 * count : 3 * count] + out[3 * count :])
            windows.append(total)
        for at, t in enumerate(tiles):
            one, two = (w[8 * at : 8 * at + 8] for w in windows)
            v, r = t // (STRIP // 2), 2 * (t % (STRIP // 2))
            yield v, r, jnp.where(first, one, pltpu.roll(two, LEVELS, 0))
            yield v, r + 1, jnp.where(first, pltpu.roll(one, LEVELS, 0), two)

    for j in range(STEPS):
        base = FIRST_FIELD[j]
        for v, r, tile in field(rep, loads[1], j, list(range(STRIP))):
            fields[base + v * (STRIP + 2 * j) + j + r] = tile
        if j > 0:
            for v, r, tile in field(sides.at[0], loads[0], j, list(range(STRIP - j, STRIP))):
                if r >= STRIP - j:
                    fields[base + v * (STRIP + 2 * j) + j + r - STRIP] = tile
            for v, r, tile in field(sides.at[1], loads[2], j, list(range(j))):
                if r < j:
                    fields[base + v * (STRIP + 2 * j) + j + r + STRIP] = tile
    for copy in copies:
        copy.wait()
    for c in range(PARTS):
        model = raw[0, c] * mult_out[c] + raw[1, c]
        model_out[c] = model if c < LEVELS else model - final0[c - LEVELS]


def adjoint_kernel(
    mult, outer, mine, outermost, back, fields,
    image,
    state, flux,
):
    def backdrop(v, row):
        if v > 0 and row in (0, EXT - 1):
            return outermost[v - 1, 1 if row else 0]
        return back[v, row]

    first = lower_half()
    half = EXT // 2
    for v in range(VARS):
        for i in range(half):
            own, after = mine[v * half + i], outer[v * half + i]
            state[0, v, i] = -jnp.where(first, own, pltpu.roll(after, LEVELS, 0))
            state[0, v, i + half] = -jnp.where(first, pltpu.roll(own, LEVELS, 0), after)
    weights = mix_weights(SCALE * coupling.T)
    for step, j in enumerate(reversed(range(STEPS))):
        now, later = state.at[step % 2], state.at[(step + 1) % 2]

        def added(v, row):
            return fields[FIRST_FIELD[j] + v * (STRIP + 2 * j) + row - step - 1]

        adjoint_step(step, now, later, backdrop, flux, weights, added)
    last = STEPS % 2
    for v in range(VARS):
        image[:, v] = mult[:, v] + state_rows(state[last, v, HALO : HALO + STRIP])


def finish_kernel(
    image, report, model, incoming, image_out, report_out, model_out, first, sems
):
    copies = [
        pltpu.make_async_copy(image, image_out, sems.at[0]),
        pltpu.make_async_copy(model.at[LEVELS:], model_out.at[LEVELS:], sems.at[1]),
        pltpu.make_async_copy(report, report_out, sems.at[2]),
        pltpu.make_async_copy(first, model_out.at[:LEVELS], sems.at[3]),
    ]
    for copy in copies[:3]:
        copy.start()
    first[...] = model[:LEVELS] - incoming[...]
    copies[3].start()
    for copy in copies:
        copy.wait()


def vmem(count):
    return [pl.BlockSpec(memory_space=pltpu.VMEM)] * count


def hbm(count):
    return [pl.BlockSpec(memory_space=pltpu.HBM)] * count


def far_from_core(x):
    return pltpu.with_memory_space_constraint(x, pltpu.HBM)


def shaped(*shape, kind=f32):
    return jax.ShapeDtypeStruct(shape, kind)


def cost(kernel_us):
    return pl.CostEstimate(flops=int(kernel_us * 1e9), bytes_accessed=int(kernel_us * 3e6), transcendentals=0)


def per_device(
    multipliers,
    increments,
    background,
    error_variance,
    report_weights,
    report_variance,
    report_cells,
    report_offsets,
    report_counts,
):
    mult, inc, bg, variance = (
        x.reshape(PARTS, VARS, STRIP, NX)
        for x in (multipliers, increments, background, error_variance)
    )
    count = lax.axis_size("space")
    wins = lax.axis_size("win")
    tile = (PARTS, NX)
    rows = shaped(VARS, STRIP, *tile)
    extended = shaped(VARS, EXT, *tile)
    whole = shaped(PARTS, VARS, STRIP, NX)
    scratch = pltpu.VMEM(whole.shape, f32)
    near, inner, rep, inc_rows, bg_rows, mult_rows = pl.pallas_call(
        pack_kernel,
        name="pack",
        out_shape=(
            shaped(NEAR, *tile),
            shaped(NEAR + FAR, *tile),
            shaped(3, *tile),
            rows,
            rows,
            rows,
        ),
        in_specs=hbm(6),
        out_specs=vmem(6),
        scratch_shapes=[
            pltpu.VMEM((3, *whole.shape), f32),
            pltpu.VMEM(report_cells.shape, jnp.int32),
            pltpu.VMEM(report_offsets.shape, f32),
            pltpu.VMEM(report_counts.shape, jnp.int32),
            pltpu.SemaphoreType.DMA((6,)),
        ],
        compiler_params=params,
    )(
        *(
            far_from_core(x)
            for x in (inc, bg, mult, report_cells, report_offsets, report_counts)
        )
    )
    both = lambda pairs: pairs + [(target, source) for source, target in pairs]
    near = lax.ppermute(near, "space", both([(i, i + 1) for i in range(1, count - 1, 2)]))
    inner = lax.ppermute(inner, "space", both([(i, i + 1) for i in range(0, count, 2)]))
    hot = shaped(2 * STEPS, NX, NX, kind=bf16)
    far, along, rests, early, known = pl.pallas_call(
        prepare_kernel,
        name="prepare",
        out_shape=(
            shaped(FAR, *tile), hot, hot, shaped(*tile), shaped(STEPS - 1, VARS, STRIP, *tile)
        ),
        in_specs=vmem(4),
        out_specs=vmem(5),
        scratch_shapes=[pltpu.VMEM((EXT, *tile), f32)],
        cost_estimate=cost(2),
        compiler_params=params,
    )(inc_rows, bg_rows, mult_rows, rep)
    far = lax.ppermute(far, "space", both([(i, i + 1) for i in range(1, count - 1, 2)]))
    final0, final1, send, expected, back = pl.pallas_call(
        tangent_kernel,
        name="tangent",
        out_shape=(
            shaped(LEVELS, VARS, STRIP, NX),
            shaped(LEVELS, VARS, STRIP, NX),
            shaped(OWNERS, 4 * CAP * PARTS),
            shaped(*tile),
            extended,
        ),
        in_specs=vmem(11),
        out_specs=vmem(2) + hbm(1) + vmem(2),
        scratch_shapes=[
            pltpu.VMEM((STEPS + 1, *extended.shape), f32),
            pltpu.VMEM((EXT, *tile), f32),
            pltpu.VMEM(tile, f32),
            pltpu.VMEM((OWNERS, 4 * CAP * PARTS), f32),
            pltpu.SemaphoreType.DMA,
        ],
        cost_estimate=cost(2),
        compiler_params=params,
    )(
        inc_rows, bg_rows, rep, along, rests, early, known, inner, near, report_weights,
        report_variance,
    )
    got = lax.all_to_all(send, "space", split_axis=0, concat_axis=0, tiled=True)
    folded = shaped(VARS * EXT // 2, *tile)
    half = shaped(LEVELS, VARS, STRIP, NX)
    outer, final1, mine, outermost, sides = pl.pallas_call(
        outer_kernel,
        name="outer",
        out_shape=(
            folded, half, folded, shaped(2, 2, *tile), shaped(2, 3, *tile)
        ),
        in_specs=vmem(4),
        out_specs=vmem(5),
        cost_estimate=cost(OUTER_COST),
        compiler_params=params,
    )(mult_rows, inner, far, final1)
    incoming = lax.ppermute(final1, "win", [(i, i + 1) for i in range(wins - 1)])
    outer = lax.ppermute(outer, "win", [(i + 1, i) for i in range(wins - 1)])
    report, fields, mult_near, model = pl.pallas_call(
        fields_kernel,
        name="fields",
        out_shape=(
            shaped(2, STEPS, NX), shaped(FIRST_FIELD[STEPS], *tile), whole, whole
        ),
        in_specs=hbm(3) + vmem(5),
        out_specs=vmem(4),
        scratch_shapes=[pltpu.VMEM((2, *whole.shape), f32), pltpu.SemaphoreType.DMA((3,))],
        cost_estimate=cost(FIELDS_COST),
        compiler_params=params,
    )(
        *(far_from_core(x) for x in (mult, variance, inc)),
        got, expected, rep, sides, final0,
    )
    image = pl.pallas_call(
        adjoint_kernel,
        name="adjoint",
        out_shape=whole,
        in_specs=vmem(6),
        out_specs=vmem(1)[0],
        scratch_shapes=[
            pltpu.VMEM((2, *extended.shape), f32),
            pltpu.VMEM(extended.shape, f32),
        ],
        cost_estimate=cost(ADJOINT_COST),
        compiler_params=params,
    )(mult_near, outer, mine, outermost, back, fields)
    image, report, model = pl.pallas_call(
        finish_kernel,
        name="finish",
        out_shape=(whole, shaped(2, STEPS, NX), whole),
        in_specs=vmem(4),
        out_specs=hbm(3),
        scratch_shapes=[pltpu.VMEM(half.shape, f32), pltpu.SemaphoreType.DMA((4,))],
        compiler_params=params,
    )(image, report, model, incoming)
    return model.reshape(multipliers.shape), report, image.reshape(multipliers.shape)


def solution(mesh):
    state = P("win", None, "space", None)
    slots = P("win", None, "space")
    return jax.shard_map(
        per_device,
        mesh=mesh,
        in_specs=(state, state, state, state, slots, slots, slots, P("win", None, None, "space"), slots),
        out_specs=(state, slots, state),
        check_vma=False,
    )
```

```python
import jax
import jax.numpy as jnp
import numpy as np
from jax import lax
from jax.experimental import pallas as pl
from jax.experimental.pallas import tpu as pltpu
from jax.sharding import PartitionSpec as P

coupling = np.array(
    [[1.0, 0.55, 0.3, 0.15], [0.5, 0.9, 0.45, 0.25], [0.3, 0.4, 0.8, 0.35], [0.1, 0.2, 0.35, 0.7]],
    np.float32,
)
LEVELS = 4
VARS = 3
STEPS = 4
STRIP = 8
HALO = 4
EXT = STRIP + 2 * HALO
NX = 256
OWNERS = 64
CAP = 4
PARTS = 8
FIELD_TILES = VARS * HALO
NEAR = FIELD_TILES + VARS * (HALO - 1)
OUTER = FIELD_TILES
REPORTS = OUTER + 2
FAR = REPORTS + 3
CODES = VARS * STRIP * LEVELS
TILES = CODES // 8
FIRST_FIELD = [VARS * sum(STRIP + 2 * i for i in range(j)) for j in range(STEPS + 1)]
FIELDS_COST = 2
OUTER_COST = 0.01
ADJOINT_COST = 30
SCALE = 0.05
f32 = jnp.float32
bf16 = jnp.bfloat16
params = pltpu.CompilerParams(vmem_limit_bytes=20 * 2**20)


def east(z):
    return pltpu.roll(z, NX - 1, 1)


def west(z):
    return pltpu.roll(z, 1, 1)


def mix_weights(matrix):
    level = lax.broadcasted_iota(jnp.int32, (PARTS, NX), 0) % LEVELS
    weights = []
    for shift in range(1 - LEVELS, LEVELS):
        weight = jnp.zeros((PARTS, NX), f32)
        for l in range(LEVELS):
            if 0 <= l + shift < LEVELS:
                weight = jnp.where(level == l, float(matrix[l, l + shift]), weight)
        weights.append((shift, weight))
    return weights


def mix(z, weights):
    total = None
    for shift, weight in weights:
        term = weight * (z if shift == 0 else pltpu.roll(z, (-shift) % PARTS, 0))
        total = term if total is None else total + term
    return total


def split(x):
    high = x.astype(bf16)
    return high, (x - high.astype(f32)).astype(bf16)


def parity():
    return lax.axis_index("space") % 2 == 0


def state_rows(block):
    return jnp.swapaxes(block, 0, 1)


def owner_of_lane():
    lane = lax.broadcasted_iota(jnp.int32, (OWNERS, NX), 1)
    return lane // CAP == lax.broadcasted_iota(jnp.int32, (OWNERS, NX), 0)


def decode(report):
    p = report.astype(jnp.int32)
    channel = p >> 11
    level = (channel * 11) >> 5
    variable = channel - 3 * level
    code = (variable * STRIP + ((p >> 8) & 7)) * LEVELS + level
    return jnp.where(p < 0, -1024, code), p & (NX - 1)


def column_weights(report, n):
    _, column = decode(report[0, n : n + 1])
    share = report[1, n : n + 1]
    place = lax.broadcasted_iota(jnp.int32, (NX, NX), 0)
    following = jnp.where(place == ((column + 1) & (NX - 1)), share, 0.0)
    return split(jnp.where(place == column, 1.0 - share, following))


def one_hot_columns(column):
    place = lax.broadcasted_iota(jnp.int32, (NX, NX), 0).astype(jnp.int16)
    here = place == jnp.broadcast_to(column, (NX, NX)).astype(jnp.int16)
    return jnp.where(here, jnp.ones((NX, NX), bf16), jnp.zeros((NX, NX), bf16))


def lower_half():
    return lax.broadcasted_iota(jnp.int32, (PARTS, NX), 0) < LEVELS


def code_tiles(rows):
    return [v * STRIP // 2 + t for v in range(VARS) for t in range(rows[0] // 2, rows[-1] // 2 + 1)]


def window_tiles(pair):
    first = lower_half()
    one = jnp.where(first, pair[0], pltpu.roll(pair[1], LEVELS, 0))
    two = jnp.where(first, pltpu.roll(pair[0], LEVELS, 0), pair[1])
    return one, two


def chosen_rows(low_end, rows, first, last):
    return jnp.where(low_end, rows[first:last], rows[STRIP - last : STRIP - first])


def near_halo(low_end, inc_rows, bg_rows, out):
    for v in range(VARS):
        at = v * HALO
        out[at : at + HALO] = chosen_rows(low_end, inc_rows[v], 0, HALO)
        at = FIELD_TILES + v * (HALO - 1)
        out[at : at + HALO - 1] = chosen_rows(low_end, bg_rows[v], 0, HALO - 1)


def far_halo(low_end, mult_rows, bg_rows, rep, out):
    for v in range(VARS):
        at = v * HALO
        out[at : at + HALO] = chosen_rows(low_end, mult_rows[v], 0, HALO)
        if v > 0:
            at = OUTER + v - 1
            out[at : at + 1] = chosen_rows(low_end, bg_rows[v], HALO - 1, HALO)
    out[REPORTS:] = rep[...]


def pack_kernel(
    inc, bg, mult, cells, offsets, counts,
    near, inner, rep, inc_rows, bg_rows, mult_rows,
    raw, raw_cells, raw_offsets, raw_counts, sems,
):
    copies = []
    for n, (source, target) in enumerate(
        (
            (inc, raw.at[0]),
            (bg, raw.at[1]),
            (mult, raw.at[2]),
            (cells, raw_cells),
            (offsets, raw_offsets),
            (counts, raw_counts),
        )
    ):
        copies.append(pltpu.make_async_copy(source, target, sems.at[n]))
        copies[n].start()
    even = parity()
    odd = jnp.logical_not(even)
    for f, rows_out in enumerate((inc_rows, bg_rows, mult_rows)):
        copies[f].wait()
        for v in range(VARS):
            rows_out[v] = state_rows(raw[f, :, v])
    near_halo(even, inc_rows, bg_rows, near)
    near_halo(odd, inc_rows, bg_rows, inner)
    for copy in copies[3:]:
        copy.wait()
    slot = lax.broadcasted_iota(jnp.int32, (PARTS, NX), 1) % CAP
    count = jnp.concatenate([raw_counts[0], raw_counts[1]], axis=0).astype(f32).astype(bf16)
    spread = jnp.where(owner_of_lane(), 1.0, 0.0).astype(f32).astype(bf16)
    live = slot.astype(f32) < jnp.dot(count, spread, preferred_element_type=f32)
    cell = jnp.concatenate([raw_cells[0], raw_cells[1]], axis=0).astype(f32)
    rep[0] = jnp.where(live, cell, -1.0)
    for k in range(2):
        for j in range(STEPS):
            for side in range(2):
                rep[1 + side, pl.ds(k * STEPS + j, 1), :] = raw_offsets[k, j, pl.ds(side, 1), :]
    far_halo(odd, mult_rows, bg_rows, rep, inner.at[NEAR:])


def sample(rows, j, rep, weights, rests, vals):
    pairs = [
        window_tiles((rows[v][r], rows[v][r + 1])) for v in range(VARS) for r in range(0, STRIP, 2)
    ]
    place = lax.broadcasted_iota(jnp.int32, (PARTS, NX), 0)
    for k in range(2):
        n = k * STEPS + j
        high, low = split(jnp.concatenate([pair[k] for pair in pairs], axis=0))
        code, _ = decode(rep[0, n : n + 1])
        picked = jnp.dot(
            jnp.concatenate([high, low], axis=0), weights[n], preferred_element_type=f32
        )
        rest = jnp.dot(high, rests[n], preferred_element_type=f32)
        sums = [jnp.zeros((PARTS, NX), f32) for _ in range(2)]
        for t in range(TILES):
            at = t * 8
            value = picked[at : at + 8] + (picked[CODES + at : CODES + at + 8] + rest[at : at + 8])
            sums = [
                jnp.where(code == place + at, value, sums[0]),
                jnp.where(code == place + (at - LEVELS), value, sums[1]),
            ]
        b = rep[2, n : n + 1]
        value = (1.0 - b) * sums[0] + b * sums[1]
        vals[pl.ds(n, 1), :] = jnp.sum(value, axis=0, keepdims=True)


def tangent_rows(get, back, raised, weights, rows, put):
    for row in sorted({near for row in rows for near in (row - 1, row, row + 1)}):
        raised[row] = mix(get(2, row), weights)
    for row in rows:
        ub, vb, hb = back(0, row), back(1, row), back(2, row)
        centre = [get(v, row) for v in range(VARS)]
        up = [get(v, row + 1) for v in range(VARS)]
        down = [get(v, row - 1) for v in range(VARS)]
        e = [east(z) for z in centre]
        w = [west(z) for z in centre]
        cols = [e[v] - w[v] for v in range(VARS)]
        slopes = [up[v] - down[v] for v in range(VARS)]
        smooth = [up[v] + down[v] + (e[v] + w[v]) for v in range(VARS)]
        lift = raised[row]
        push_c = east(lift) - west(lift)
        push_r = raised[row + 1] - raised[row - 1]
        new = [
            0.98 * centre[0]
            + 0.03 * centre[1]
            + 0.005 * smooth[0]
            - push_c
            - (ub * cols[0] + vb * slopes[0]),
            0.98 * centre[1]
            - 0.03 * centre[0]
            + 0.005 * smooth[1]
            - push_r
            - (ub * cols[1] + vb * slopes[1]),
            0.98 * centre[2]
            + 0.005 * smooth[2]
            - hb * (cols[0] + slopes[1])
            - (ub * cols[2] + vb * slopes[2]),
        ]
        for v in range(VARS):
            put(v, row, new[v])


def inside(step):
    return range(HALO + 1 + step, HALO + STRIP - 1 - step)


def prepare_kernel(
    inc_rows, bg_rows, mult_rows, rep, far, along, rests, vals, known, raised
):
    far_halo(parity(), mult_rows, bg_rows, rep, far)
    for n in range(2 * STEPS):
        along[n], rests[n] = column_weights(rep, n)
    vals[...] = jnp.zeros((PARTS, NX), f32)
    rows = [[inc_rows[v, r] for r in range(STRIP)] for v in range(VARS)]
    sample(rows, 0, rep, along, rests, vals)
    weights = mix_weights(SCALE * coupling)
    for step in range(STEPS - 1):
        before = inc_rows if step == 0 else known.at[step - 1]

        def put(v, row, value):
            known[step, v, row - HALO] = value

        tangent_rows(
            lambda v, row: before[v, row - HALO],
            lambda v, row: SCALE * bg_rows[v, row - HALO],
            raised,
            weights,
            inside(step),
            put,
        )


def edges():
    s = lax.axis_index("space")
    top = jnp.where(s > 0, 1.0, 0.0).astype(f32)
    bottom = jnp.where(s < OWNERS - 1, 1.0, 0.0).astype(f32)
    return top, bottom


def both_sides(even, a, b):
    return jnp.where(even, b, a), jnp.where(even, a, b)


def send_out(vals, owned, owned_variance, expected, send, packed, sem):
    own = jnp.concatenate([owned[0], owned[1]], axis=0)
    expected[...] = own * jnp.concatenate([owned_variance[0], owned_variance[1]], axis=0)
    slot = lax.broadcasted_iota(jnp.int32, (PARTS, NX), 1) % CAP
    pieces = []
    for piece in (pltpu.roll(own, CAP, 1), own, pltpu.roll(own, NX - CAP, 1), vals[...]):
        for i in range(CAP):
            pieces.append(jnp.where(slot == i, piece, 0.0))
    chosen = jnp.where(owner_of_lane(), 1.0, 0.0).astype(f32).astype(bf16)
    both = lax.dot_general(
        chosen,
        jnp.concatenate(split(jnp.concatenate(pieces, axis=0)), axis=0),
        (((1,), (1,)), ((), ())),
        preferred_element_type=f32,
    )
    lanes = 4 * CAP * PARTS
    packed[...] = both[:, :lanes] + both[:, lanes:]
    copy = pltpu.make_async_copy(packed, send, sem)
    copy.start()
    return copy


def tangent_kernel(
    inc_rows, bg_rows, rep, along, rests, early, known, got_a, got_near, owned, owned_variance,
    final0, final1, send, expected, back,
    state, raised, vals, packed, sem,
):
    even = parity()
    top, bottom = edges()
    end = HALO + STRIP
    for v in range(VARS):
        at = v * HALO
        low, high = both_sides(even, got_a[at : at + HALO], got_near[at : at + HALO])
        state[0, v, :HALO] = low
        state[0, v, end:] = high
        at = FIELD_TILES + v * (HALO - 1)
        low, high = both_sides(even, got_a[at : at + HALO - 1], got_near[at : at + HALO - 1])
        back[v, 1:HALO] = SCALE * low
        back[v, HALO:end] = SCALE * bg_rows[v]
        back[v, end : EXT - 1] = SCALE * high
        back[v, 0] = jnp.zeros((PARTS, NX), f32)
        back[v, EXT - 1] = jnp.zeros((PARTS, NX), f32)

    weights = mix_weights(SCALE * coupling)
    vals[...] = early[...]

    def get_at(j, v, row):
        if j == 0 and HALO <= row < end:
            return inc_rows[v, row - HALO]
        if j > 0 and row in inside(j - 1):
            return known[j - 1, v, row - HALO]
        return state[j, v, row]

    def advance(j, rows):
        def put(v, row, value):
            if row < HALO:
                value = value * top
            elif row >= end:
                value = value * bottom
            state[j + 1, v, row] = value

        tangent_rows(
            lambda v, row: get_at(j, v, row), lambda v, row: back[v, row], raised, weights, rows, put
        )

    for j in range(STEPS - 1):
        advance(j, [row for row in range(j + 2, EXT - 2 - j) if row not in inside(j)])
        rows = [[get_at(j + 1, v, HALO + r) for r in range(STRIP)] for v in range(VARS)]
        sample(rows, j + 1, rep, along, rests, vals)
    copy = send_out(vals, owned, owned_variance, expected, send, packed, sem)
    @pl.when(lax.axis_index("space") >= 0)
    def while_it_leaves():
        for j in range(STEPS - 1):
            advance(j, [j + 1, EXT - 2 - j])
        advance(STEPS - 1, list(range(HALO, end)))
        last = STEPS
        for v in range(VARS):
            value = state_rows(state[last, v, HALO : HALO + STRIP])
            final0[:, v] = value[:LEVELS]
            final1[:, v] = value[LEVELS:]

    copy.wait()


def outer_kernel(mult_rows, inner, far, final1, out, final_out, mine, outermost, sides):
    even = parity()
    half = EXT // 2
    final_out[...] = final1[...]
    for v in range(VARS):
        at = v * HALO
        low, high = both_sides(
            even, inner[NEAR + at : NEAR + at + HALO], far[at : at + HALO]
        )
        rows = (
            [low[i] for i in range(HALO)]
            + [mult_rows[v, r] for r in range(STRIP)]
            + [high[i] for i in range(HALO)]
        )
        for i in range(half):
            n = v * half + i
            out[n], mine[n] = window_tiles((rows[i], rows[i + half]))
    for v in (1, 2):
        at = OUTER + v - 1
        low, high = both_sides(even, inner[NEAR + at], far[at])
        outermost[v - 1, 0], outermost[v - 1, 1] = SCALE * low, SCALE * high
    for n in range(3):
        at = REPORTS + n
        sides[0, n], sides[1, n] = both_sides(even, inner[NEAR + at], far[at])


def adjoint_step(step, now, later, back, flux, weights, added):
    top, bottom = edges()
    for row in range(step, EXT - step):
        vb, hb = back(1, row), back(2, row)
        au, av, ah = now[0, row], now[1, row], now[2, row]
        flux[0, row] = vb * au
        flux[1, row] = hb * ah + vb * av
        flux[2, row] = vb * ah
    for row in range(step + 1, EXT - 1 - step):
        ub, hb = back(0, row), back(2, row)
        centre = [now[v, row] for v in range(VARS)]
        au, av, ah = centre
        across = [hb * ah + ub * au, ub * av, ub * ah]
        lift = mix((east(au) - west(au)) + (now[1, row + 1] - now[1, row - 1]), weights)
        turn = [0.98 * au - 0.03 * av, 0.98 * av + 0.03 * au, 0.98 * ah + lift]
        for v in range(VARS):
            spread = 0.005 * centre[v]
            value = (
                turn[v]
                + (east(spread + across[v]) + west(spread - across[v]))
                + (0.005 * (now[v, row + 1] + now[v, row - 1]) + (flux[v, row + 1] - flux[v, row - 1]))
            )
            value = value + added(v, row)
            if row < HALO:
                value = value * top
            elif row >= HALO + STRIP:
                value = value * bottom
            later[v, row] = value


def fields_kernel(
    mult, variance, inc, got, expected, rep, sides, final0,
    report_out, fields, mult_out, model_out,
    raw, sems,
):
    copies = []
    for n, (source, target) in enumerate(
        ((mult, mult_out), (variance, raw.at[0]), (inc, raw.at[1]))
    ):
        copies.append(pltpu.make_async_copy(source, target, sems.at[n]))
        copies[n].start()
    chosen = jnp.where(owner_of_lane(), 1.0, 0.0).astype(f32).astype(bf16)
    spread = jnp.dot(
        jnp.concatenate(split(jnp.transpose(got[...])), axis=0),
        chosen,
        preferred_element_type=f32,
    )
    lanes = 4 * CAP * PARTS
    spread = spread[:lanes] + spread[lanes:]
    slot = lax.broadcasted_iota(jnp.int32, (PARTS, NX), 1) % CAP
    loads = []
    for g in range(4):
        value = jnp.zeros((PARTS, NX), f32)
        for i in range(CAP):
            at = (g * CAP + i) * PARTS
            value = jnp.where(slot == i, spread[at : at + PARTS], value)
        loads.append(value)
    for k in range(2):
        at = k * STEPS
        report_out[k] = expected[pl.ds(at, STEPS), :] + loads[3][at : at + STEPS]
    place = lax.broadcasted_iota(jnp.int32, (PARTS, NX), 0)
    first = lower_half()
    transposed = (((1,), (1,)), ((), ()))

    def field(report, load, j, rows):
        tiles = code_tiles(rows)
        count = 8 * len(tiles)
        windows = []
        for k in range(2):
            n = k * STEPS + j
            code, column = decode(report[0, n : n + 1])
            a, b = report[1, n : n + 1], report[2, n : n + 1]
            weight = load[n : n + 1]
            parts = []
            for share in ((1.0 - a) * weight, a * weight):
                own, following = (1.0 - b) * share, b * share
                block = []
                for t in tiles:
                    tile = jnp.where(code == place + (8 * t - LEVELS), following, 0.0)
                    block.append(jnp.where(code == place + 8 * t, own, tile))
                parts += list(split(jnp.concatenate(block, axis=0)))
            out = lax.dot_general(
                jnp.concatenate(parts, axis=0),
                one_hot_columns(column),
                transposed,
                preferred_element_type=f32,
            )
            total = out[:count] + out[count : 2 * count]
            total = total + west(out[2 * count : 3 * count] + out[3 * count :])
            windows.append(total)
        for at, t in enumerate(tiles):
            one, two = (w[8 * at : 8 * at + 8] for w in windows)
            v, r = t // (STRIP // 2), 2 * (t % (STRIP // 2))
            yield v, r, jnp.where(first, one, pltpu.roll(two, LEVELS, 0))
            yield v, r + 1, jnp.where(first, pltpu.roll(one, LEVELS, 0), two)

    for j in range(STEPS):
        base = FIRST_FIELD[j]
        for v, r, tile in field(rep, loads[1], j, list(range(STRIP))):
            fields[base + v * (STRIP + 2 * j) + j + r] = tile
        if j > 0:
            for v, r, tile in field(sides.at[0], loads[0], j, list(range(STRIP - j, STRIP))):
                if r >= STRIP - j:
                    fields[base + v * (STRIP + 2 * j) + j + r - STRIP] = tile
            for v, r, tile in field(sides.at[1], loads[2], j, list(range(j))):
                if r < j:
                    fields[base + v * (STRIP + 2 * j) + j + r + STRIP] = tile
    for copy in copies:
        copy.wait()
    for c in range(PARTS):
        model = raw[0, c] * mult_out[c] + raw[1, c]
        model_out[c] = model if c < LEVELS else model - final0[c - LEVELS]


def adjoint_kernel(
    mult, outer, mine, outermost, back, fields,
    image,
    state, flux,
):
    def backdrop(v, row):
        if v > 0 and row in (0, EXT - 1):
            return outermost[v - 1, 1 if row else 0]
        return back[v, row]

    first = lower_half()
    half = EXT // 2
    for v in range(VARS):
        for i in range(half):
            own, after = mine[v * half + i], outer[v * half + i]
            state[0, v, i] = -jnp.where(first, own, pltpu.roll(after, LEVELS, 0))
            state[0, v, i + half] = -jnp.where(first, pltpu.roll(own, LEVELS, 0), after)
    weights = mix_weights(SCALE * coupling.T)
    for step, j in enumerate(reversed(range(STEPS))):
        now, later = state.at[step % 2], state.at[(step + 1) % 2]

        def added(v, row):
            return fields[FIRST_FIELD[j] + v * (STRIP + 2 * j) + row - step - 1]

        adjoint_step(step, now, later, backdrop, flux, weights, added)
    last = STEPS % 2
    for v in range(VARS):
        image[:, v] = mult[:, v] + state_rows(state[last, v, HALO : HALO + STRIP])


def finish_kernel(
    image, report, model, incoming, image_out, report_out, model_out, first, sems
):
    copies = [
        pltpu.make_async_copy(image, image_out, sems.at[0]),
        pltpu.make_async_copy(model.at[LEVELS:], model_out.at[LEVELS:], sems.at[1]),
        pltpu.make_async_copy(report, report_out, sems.at[2]),
        pltpu.make_async_copy(first, model_out.at[:LEVELS], sems.at[3]),
    ]
    for copy in copies[:3]:
        copy.start()
    first[...] = model[:LEVELS] - incoming[...]
    copies[3].start()
    for copy in copies:
        copy.wait()


def vmem(count):
    return [pl.BlockSpec(memory_space=pltpu.VMEM)] * count


def hbm(count):
    return [pl.BlockSpec(memory_space=pltpu.HBM)] * count


def far_from_core(x):
    return pltpu.with_memory_space_constraint(x, pltpu.HBM)


def shaped(*shape, kind=f32):
    return jax.ShapeDtypeStruct(shape, kind)


def cost(kernel_us):
    return pl.CostEstimate(flops=int(kernel_us * 1e9), bytes_accessed=int(kernel_us * 3e6), transcendentals=0)


def per_device(
    multipliers,
    increments,
    background,
    error_variance,
    report_weights,
    report_variance,
    report_cells,
    report_offsets,
    report_counts,
):
    mult, inc, bg, variance = (
        x.reshape(PARTS, VARS, STRIP, NX)
        for x in (multipliers, increments, background, error_variance)
    )
    count = lax.axis_size("space")
    wins = lax.axis_size("win")
    tile = (PARTS, NX)
    rows = shaped(VARS, STRIP, *tile)
    extended = shaped(VARS, EXT, *tile)
    whole = shaped(PARTS, VARS, STRIP, NX)
    scratch = pltpu.VMEM(whole.shape, f32)
    near, inner, rep, inc_rows, bg_rows, mult_rows = pl.pallas_call(
        pack_kernel,
        name="pack",
        out_shape=(
            shaped(NEAR, *tile),
            shaped(NEAR + FAR, *tile),
            shaped(3, *tile),
            rows,
            rows,
            rows,
        ),
        in_specs=hbm(6),
        out_specs=vmem(6),
        scratch_shapes=[
            pltpu.VMEM((3, *whole.shape), f32),
            pltpu.VMEM(report_cells.shape, jnp.int32),
            pltpu.VMEM(report_offsets.shape, f32),
            pltpu.VMEM(report_counts.shape, jnp.int32),
            pltpu.SemaphoreType.DMA((6,)),
        ],
        compiler_params=params,
    )(
        *(
            far_from_core(x)
            for x in (inc, bg, mult, report_cells, report_offsets, report_counts)
        )
    )
    both = lambda pairs: pairs + [(target, source) for source, target in pairs]
    near = lax.ppermute(near, "space", both([(i, i + 1) for i in range(1, count - 1, 2)]))
    inner = lax.ppermute(inner, "space", both([(i, i + 1) for i in range(0, count, 2)]))
    hot = shaped(2 * STEPS, NX, NX, kind=bf16)
    far, along, rests, early, known = pl.pallas_call(
        prepare_kernel,
        name="prepare",
        out_shape=(
            shaped(FAR, *tile), hot, hot, shaped(*tile), shaped(STEPS - 1, VARS, STRIP, *tile)
        ),
        in_specs=vmem(4),
        out_specs=vmem(5),
        scratch_shapes=[pltpu.VMEM((EXT, *tile), f32)],
        cost_estimate=cost(2),
        compiler_params=params,
    )(inc_rows, bg_rows, mult_rows, rep)
    far = lax.ppermute(far, "space", both([(i, i + 1) for i in range(1, count - 1, 2)]))
    final0, final1, send, expected, back = pl.pallas_call(
        tangent_kernel,
        name="tangent",
        out_shape=(
            shaped(LEVELS, VARS, STRIP, NX),
            shaped(LEVELS, VARS, STRIP, NX),
            shaped(OWNERS, 4 * CAP * PARTS),
            shaped(*tile),
            extended,
        ),
        in_specs=vmem(11),
        out_specs=vmem(2) + hbm(1) + vmem(2),
        scratch_shapes=[
            pltpu.VMEM((STEPS + 1, *extended.shape), f32),
            pltpu.VMEM((EXT, *tile), f32),
            pltpu.VMEM(tile, f32),
            pltpu.VMEM((OWNERS, 4 * CAP * PARTS), f32),
            pltpu.SemaphoreType.DMA,
        ],
        cost_estimate=cost(2),
        compiler_params=params,
    )(
        inc_rows, bg_rows, rep, along, rests, early, known, inner, near, report_weights,
        report_variance,
    )
    got = lax.all_to_all(send, "space", split_axis=0, concat_axis=0, tiled=True)
    folded = shaped(VARS * EXT // 2, *tile)
    half = shaped(LEVELS, VARS, STRIP, NX)
    outer, final1, mine, outermost, sides = pl.pallas_call(
        outer_kernel,
        name="outer",
        out_shape=(
            folded, half, folded, shaped(2, 2, *tile), shaped(2, 3, *tile)
        ),
        in_specs=vmem(4),
        out_specs=vmem(5),
        cost_estimate=cost(OUTER_COST),
        compiler_params=params,
    )(mult_rows, inner, far, final1)
    incoming = lax.ppermute(final1, "win", [(i, i + 1) for i in range(wins - 1)])
    outer = lax.ppermute(outer, "win", [(i + 1, i) for i in range(wins - 1)])
    report, fields, mult_near, model = pl.pallas_call(
        fields_kernel,
        name="fields",
        out_shape=(
            shaped(2, STEPS, NX), shaped(FIRST_FIELD[STEPS], *tile), whole, whole
        ),
        in_specs=hbm(3) + vmem(5),
        out_specs=vmem(4),
        scratch_shapes=[pltpu.VMEM((2, *whole.shape), f32), pltpu.SemaphoreType.DMA((3,))],
        cost_estimate=cost(FIELDS_COST),
        compiler_params=params,
    )(
        *(far_from_core(x) for x in (mult, variance, inc)),
        got, expected, rep, sides, final0,
    )
    image = pl.pallas_call(
        adjoint_kernel,
        name="adjoint",
        out_shape=whole,
        in_specs=vmem(6),
        out_specs=vmem(1)[0],
        scratch_shapes=[
            pltpu.VMEM((2, *extended.shape), f32),
            pltpu.VMEM(extended.shape, f32),
        ],
        cost_estimate=cost(ADJOINT_COST),
        compiler_params=params,
    )(mult_near, outer, mine, outermost, back, fields)
    image, report, model = pl.pallas_call(
        finish_kernel,
        name="finish",
        out_shape=(whole, shaped(2, STEPS, NX), whole),
        in_specs=vmem(4),
        out_specs=hbm(3),
        scratch_shapes=[pltpu.VMEM(half.shape, f32), pltpu.SemaphoreType.DMA((4,))],
        compiler_params=params,
    )(image, report, model, incoming)
    return model.reshape(multipliers.shape), report, image.reshape(multipliers.shape)


def solution(mesh):
    state = P("win", None, "space", None)
    slots = P("win", None, "space")
    return jax.shard_map(
        per_device,
        mesh=mesh,
        in_specs=(state, state, state, state, slots, slots, slots, P("win", None, None, "space"), slots),
        out_specs=(state, slots, state),
        check_vma=False,
    )
```

```python
import jax
import jax.numpy as jnp
import numpy as np
from jax import lax
from jax.experimental import pallas as pl
from jax.experimental.pallas import tpu as pltpu
from jax.sharding import PartitionSpec as P

coupling = np.array(
    [[1.0, 0.55, 0.3, 0.15], [0.5, 0.9, 0.45, 0.25], [0.3, 0.4, 0.8, 0.35], [0.1, 0.2, 0.35, 0.7]],
    np.float32,
)
LEVELS = 4
VARS = 3
STEPS = 4
STRIP = 8
HALO = 4
EXT = STRIP + 2 * HALO
NX = 256
OWNERS = 64
CAP = 4
PARTS = 8
FIELD_TILES = VARS * HALO
NEAR = FIELD_TILES + VARS * (HALO - 1)
OUTER = FIELD_TILES
REPORTS = OUTER + 2
FAR = REPORTS + 3
CODES = VARS * STRIP * LEVELS
TILES = CODES // 8
FIRST_FIELD = [VARS * sum(STRIP + 2 * i for i in range(j)) for j in range(STEPS + 1)]
FIELDS_COST = 2
OUTER_COST = 0.01
ADJOINT_COST = 30
SCALE = 0.05
f32 = jnp.float32
bf16 = jnp.bfloat16
params = pltpu.CompilerParams(vmem_limit_bytes=20 * 2**20)


def east(z):
    return pltpu.roll(z, NX - 1, 1)


def west(z):
    return pltpu.roll(z, 1, 1)


def mix_weights(matrix):
    level = lax.broadcasted_iota(jnp.int32, (PARTS, NX), 0) % LEVELS
    weights = []
    for shift in range(1 - LEVELS, LEVELS):
        weight = jnp.zeros((PARTS, NX), f32)
        for l in range(LEVELS):
            if 0 <= l + shift < LEVELS:
                weight = jnp.where(level == l, float(matrix[l, l + shift]), weight)
        weights.append((shift, weight))
    return weights


def mix(z, weights):
    total = None
    for shift, weight in weights:
        term = weight * (z if shift == 0 else pltpu.roll(z, (-shift) % PARTS, 0))
        total = term if total is None else total + term
    return total


def split(x):
    high = x.astype(bf16)
    return high, (x - high.astype(f32)).astype(bf16)


def parity():
    return lax.axis_index("space") % 2 == 0


def state_rows(block):
    return jnp.swapaxes(block, 0, 1)


def owner_of_lane():
    lane = lax.broadcasted_iota(jnp.int32, (OWNERS, NX), 1)
    return lane // CAP == lax.broadcasted_iota(jnp.int32, (OWNERS, NX), 0)


def decode(report):
    p = report.astype(jnp.int32)
    channel = p >> 11
    level = (channel * 11) >> 5
    variable = channel - 3 * level
    code = (variable * STRIP + ((p >> 8) & 7)) * LEVELS + level
    return jnp.where(p < 0, -1024, code), p & (NX - 1)


def column_weights(report, n):
    _, column = decode(report[0, n : n + 1])
    share = report[1, n : n + 1]
    place = lax.broadcasted_iota(jnp.int32, (NX, NX), 0).astype(jnp.int16)

    def spread(row, kind):
        return jnp.broadcast_to(row, (NX, NX)).astype(kind)

    here = place == spread(column, jnp.int16)
    following = place == spread((column + 1) & (NX - 1), jnp.int16)
    none = jnp.zeros((NX, NX), bf16)
    return [
        jnp.where(here, spread(own, bf16), jnp.where(following, spread(other, bf16), none))
        for own, other in zip(
            (x.astype(f32) for x in split(1.0 - share)), (x.astype(f32) for x in split(share))
        )
    ]


def one_hot_columns(column):
    place = lax.broadcasted_iota(jnp.int32, (NX, NX), 0).astype(jnp.int16)
    here = place == jnp.broadcast_to(column, (NX, NX)).astype(jnp.int16)
    return jnp.where(here, jnp.ones((NX, NX), bf16), jnp.zeros((NX, NX), bf16))


def lower_half():
    return lax.broadcasted_iota(jnp.int32, (PARTS, NX), 0) < LEVELS


def code_tiles(rows):
    return [v * STRIP // 2 + t for v in range(VARS) for t in range(rows[0] // 2, rows[-1] // 2 + 1)]


def window_tiles(pair):
    first = lower_half()
    one = jnp.where(first, pair[0], pltpu.roll(pair[1], LEVELS, 0))
    two = jnp.where(first, pltpu.roll(pair[0], LEVELS, 0), pair[1])
    return one, two


def chosen_rows(low_end, rows, first, last):
    return jnp.where(low_end, rows[first:last], rows[STRIP - last : STRIP - first])


def near_halo(low_end, inc_rows, bg_rows, out):
    for v in range(VARS):
        at = v * HALO
        out[at : at + HALO] = chosen_rows(low_end, inc_rows[v], 0, HALO)
        at = FIELD_TILES + v * (HALO - 1)
        out[at : at + HALO - 1] = chosen_rows(low_end, bg_rows[v], 0, HALO - 1)


def far_halo(low_end, mult_rows, bg_rows, rep, out):
    for v in range(VARS):
        at = v * HALO
        out[at : at + HALO] = chosen_rows(low_end, mult_rows[v], 0, HALO)
        if v > 0:
            at = OUTER + v - 1
            out[at : at + 1] = chosen_rows(low_end, bg_rows[v], HALO - 1, HALO)
    out[REPORTS:] = rep[...]


def pack_kernel(
    inc, bg, mult, cells, offsets, counts,
    near, inner, rep, inc_rows, bg_rows, mult_rows,
    raw, raw_cells, raw_offsets, raw_counts, sems,
):
    copies = []
    for n, (source, target) in enumerate(
        (
            (inc, raw.at[0]),
            (bg, raw.at[1]),
            (mult, raw.at[2]),
            (cells, raw_cells),
            (offsets, raw_offsets),
            (counts, raw_counts),
        )
    ):
        copies.append(pltpu.make_async_copy(source, target, sems.at[n]))
        copies[n].start()
    even = parity()
    odd = jnp.logical_not(even)
    for f, rows_out in enumerate((inc_rows, bg_rows, mult_rows)):
        copies[f].wait()
        for v in range(VARS):
            rows_out[v] = state_rows(raw[f, :, v])
    near_halo(even, inc_rows, bg_rows, near)
    near_halo(odd, inc_rows, bg_rows, inner)
    for copy in copies[3:]:
        copy.wait()
    slot = lax.broadcasted_iota(jnp.int32, (PARTS, NX), 1) % CAP
    count = jnp.concatenate([raw_counts[0], raw_counts[1]], axis=0).astype(f32).astype(bf16)
    spread = jnp.where(owner_of_lane(), 1.0, 0.0).astype(f32).astype(bf16)
    live = slot.astype(f32) < jnp.dot(count, spread, preferred_element_type=f32)
    cell = jnp.concatenate([raw_cells[0], raw_cells[1]], axis=0).astype(f32)
    rep[0] = jnp.where(live, cell, -1.0)
    for k in range(2):
        for j in range(STEPS):
            for side in range(2):
                rep[1 + side, pl.ds(k * STEPS + j, 1), :] = raw_offsets[k, j, pl.ds(side, 1), :]
    far_halo(odd, mult_rows, bg_rows, rep, inner.at[NEAR:])


def sample(rows, j, rep, weights, rests, vals):
    pairs = [
        window_tiles((rows[v][r], rows[v][r + 1])) for v in range(VARS) for r in range(0, STRIP, 2)
    ]
    place = lax.broadcasted_iota(jnp.int32, (PARTS, NX), 0)
    for k in range(2):
        n = k * STEPS + j
        high, low = split(jnp.concatenate([pair[k] for pair in pairs], axis=0))
        code, _ = decode(rep[0, n : n + 1])
        picked = jnp.dot(
            jnp.concatenate([high, low], axis=0), weights[n], preferred_element_type=f32
        )
        rest = jnp.dot(high, rests[n], preferred_element_type=f32)
        sums = [jnp.zeros((PARTS, NX), f32) for _ in range(2)]
        for t in range(TILES):
            at = t * 8
            value = picked[at : at + 8] + (picked[CODES + at : CODES + at + 8] + rest[at : at + 8])
            sums = [
                jnp.where(code == place + at, value, sums[0]),
                jnp.where(code == place + (at - LEVELS), value, sums[1]),
            ]
        b = rep[2, n : n + 1]
        value = (1.0 - b) * sums[0] + b * sums[1]
        vals[pl.ds(n, 1), :] = jnp.sum(value, axis=0, keepdims=True)


def tangent_rows(get, back, raised, weights, rows, put):
    for row in sorted({near for row in rows for near in (row - 1, row, row + 1)}):
        raised[row] = mix(get(2, row), weights)
    for row in rows:
        ub, vb, hb = back(0, row), back(1, row), back(2, row)
        centre = [get(v, row) for v in range(VARS)]
        up = [get(v, row + 1) for v in range(VARS)]
        down = [get(v, row - 1) for v in range(VARS)]
        e = [east(z) for z in centre]
        w = [west(z) for z in centre]
        cols = [e[v] - w[v] for v in range(VARS)]
        slopes = [up[v] - down[v] for v in range(VARS)]
        smooth = [up[v] + down[v] + (e[v] + w[v]) for v in range(VARS)]
        lift = raised[row]
        push_c = east(lift) - west(lift)
        push_r = raised[row + 1] - raised[row - 1]
        new = [
            0.98 * centre[0]
            + 0.03 * centre[1]
            + 0.005 * smooth[0]
            - push_c
            - (ub * cols[0] + vb * slopes[0]),
            0.98 * centre[1]
            - 0.03 * centre[0]
            + 0.005 * smooth[1]
            - push_r
            - (ub * cols[1] + vb * slopes[1]),
            0.98 * centre[2]
            + 0.005 * smooth[2]
            - hb * (cols[0] + slopes[1])
            - (ub * cols[2] + vb * slopes[2]),
        ]
        for v in range(VARS):
            put(v, row, new[v])


def inside(step):
    return range(HALO + 1 + step, HALO + STRIP - 1 - step)


def prepare_kernel(
    inc_rows, bg_rows, mult_rows, rep, far, along, rests, vals, known, raised
):
    far_halo(parity(), mult_rows, bg_rows, rep, far)
    for n in range(2 * STEPS):
        along[n], rests[n] = column_weights(rep, n)
    vals[...] = jnp.zeros((PARTS, NX), f32)
    rows = [[inc_rows[v, r] for r in range(STRIP)] for v in range(VARS)]
    sample(rows, 0, rep, along, rests, vals)
    weights = mix_weights(SCALE * coupling)
    for step in range(STEPS - 1):
        before = inc_rows if step == 0 else known.at[step - 1]

        def put(v, row, value):
            known[step, v, row - HALO] = value

        tangent_rows(
            lambda v, row: before[v, row - HALO],
            lambda v, row: SCALE * bg_rows[v, row - HALO],
            raised,
            weights,
            inside(step),
            put,
        )


def edges():
    s = lax.axis_index("space")
    top = jnp.where(s > 0, 1.0, 0.0).astype(f32)
    bottom = jnp.where(s < OWNERS - 1, 1.0, 0.0).astype(f32)
    return top, bottom


def both_sides(even, a, b):
    return jnp.where(even, b, a), jnp.where(even, a, b)


def send_out(vals, owned, owned_variance, expected, send, packed, sem):
    own = jnp.concatenate([owned[0], owned[1]], axis=0)
    expected[...] = own * jnp.concatenate([owned_variance[0], owned_variance[1]], axis=0)
    slot = lax.broadcasted_iota(jnp.int32, (PARTS, NX), 1) % CAP
    pieces = []
    for piece in (pltpu.roll(own, CAP, 1), own, pltpu.roll(own, NX - CAP, 1), vals[...]):
        for i in range(CAP):
            pieces.append(jnp.where(slot == i, piece, 0.0))
    chosen = jnp.where(owner_of_lane(), 1.0, 0.0).astype(f32).astype(bf16)
    both = lax.dot_general(
        chosen,
        jnp.concatenate(split(jnp.concatenate(pieces, axis=0)), axis=0),
        (((1,), (1,)), ((), ())),
        preferred_element_type=f32,
    )
    lanes = 4 * CAP * PARTS
    packed[...] = both[:, :lanes] + both[:, lanes:]
    copy = pltpu.make_async_copy(packed, send, sem)
    copy.start()
    return copy


def tangent_kernel(
    inc_rows, bg_rows, rep, along, rests, early, known, got_a, got_near, owned, owned_variance,
    final0, final1, send, expected, back,
    state, raised, vals, packed, sem,
):
    even = parity()
    top, bottom = edges()
    end = HALO + STRIP
    for v in range(VARS):
        at = v * HALO
        low, high = both_sides(even, got_a[at : at + HALO], got_near[at : at + HALO])
        state[0, v, :HALO] = low
        state[0, v, end:] = high
        at = FIELD_TILES + v * (HALO - 1)
        low, high = both_sides(even, got_a[at : at + HALO - 1], got_near[at : at + HALO - 1])
        back[v, 1:HALO] = SCALE * low
        back[v, HALO:end] = SCALE * bg_rows[v]
        back[v, end : EXT - 1] = SCALE * high
        back[v, 0] = jnp.zeros((PARTS, NX), f32)
        back[v, EXT - 1] = jnp.zeros((PARTS, NX), f32)

    weights = mix_weights(SCALE * coupling)
    vals[...] = early[...]

    def get_at(j, v, row):
        if j == 0 and HALO <= row < end:
            return inc_rows[v, row - HALO]
        if j > 0 and row in inside(j - 1):
            return known[j - 1, v, row - HALO]
        return state[j, v, row]

    def advance(j, rows):
        def put(v, row, value):
            if row < HALO:
                value = value * top
            elif row >= end:
                value = value * bottom
            state[j + 1, v, row] = value

        tangent_rows(
            lambda v, row: get_at(j, v, row), lambda v, row: back[v, row], raised, weights, rows, put
        )

    for j in range(STEPS - 1):
        advance(j, [row for row in range(j + 2, EXT - 2 - j) if row not in inside(j)])
        rows = [[get_at(j + 1, v, HALO + r) for r in range(STRIP)] for v in range(VARS)]
        sample(rows, j + 1, rep, along, rests, vals)
    copy = send_out(vals, owned, owned_variance, expected, send, packed, sem)
    @pl.when(lax.axis_index("space") >= 0)
    def while_it_leaves():
        for j in range(STEPS - 1):
            advance(j, [j + 1, EXT - 2 - j])
        advance(STEPS - 1, list(range(HALO, end)))
        last = STEPS
        for v in range(VARS):
            value = state_rows(state[last, v, HALO : HALO + STRIP])
            final0[:, v] = value[:LEVELS]
            final1[:, v] = value[LEVELS:]

    copy.wait()


def outer_kernel(mult_rows, inner, far, final1, out, final_out, mine, outermost, sides):
    even = parity()
    half = EXT // 2
    final_out[...] = final1[...]
    for v in range(VARS):
        at = v * HALO
        low, high = both_sides(
            even, inner[NEAR + at : NEAR + at + HALO], far[at : at + HALO]
        )
        rows = (
            [low[i] for i in range(HALO)]
            + [mult_rows[v, r] for r in range(STRIP)]
            + [high[i] for i in range(HALO)]
        )
        for i in range(half):
            n = v * half + i
            out[n], mine[n] = window_tiles((rows[i], rows[i + half]))
    for v in (1, 2):
        at = OUTER + v - 1
        low, high = both_sides(even, inner[NEAR + at], far[at])
        outermost[v - 1, 0], outermost[v - 1, 1] = SCALE * low, SCALE * high
    for n in range(3):
        at = REPORTS + n
        sides[0, n], sides[1, n] = both_sides(even, inner[NEAR + at], far[at])


def adjoint_step(step, now, later, back, flux, weights, added):
    top, bottom = edges()
    for row in range(step, EXT - step):
        vb, hb = back(1, row), back(2, row)
        au, av, ah = now[0, row], now[1, row], now[2, row]
        flux[0, row] = vb * au
        flux[1, row] = hb * ah + vb * av
        flux[2, row] = vb * ah
    for row in range(step + 1, EXT - 1 - step):
        ub, hb = back(0, row), back(2, row)
        centre = [now[v, row] for v in range(VARS)]
        au, av, ah = centre
        across = [hb * ah + ub * au, ub * av, ub * ah]
        lift = mix((east(au) - west(au)) + (now[1, row + 1] - now[1, row - 1]), weights)
        turn = [0.98 * au - 0.03 * av, 0.98 * av + 0.03 * au, 0.98 * ah + lift]
        for v in range(VARS):
            spread = 0.005 * centre[v]
            value = (
                turn[v]
                + (east(spread + across[v]) + west(spread - across[v]))
                + (0.005 * (now[v, row + 1] + now[v, row - 1]) + (flux[v, row + 1] - flux[v, row - 1]))
            )
            value = value + added(v, row)
            if row < HALO:
                value = value * top
            elif row >= HALO + STRIP:
                value = value * bottom
            later[v, row] = value


def fields_kernel(
    mult, variance, inc, got, expected, rep, sides, final0,
    report_out, fields, mult_out, model_out,
    raw, sems,
):
    copies = []
    for n, (source, target) in enumerate(
        ((mult, mult_out), (variance, raw.at[0]), (inc, raw.at[1]))
    ):
        copies.append(pltpu.make_async_copy(source, target, sems.at[n]))
        copies[n].start()
    chosen = jnp.where(owner_of_lane(), 1.0, 0.0).astype(f32).astype(bf16)
    spread = jnp.dot(
        jnp.concatenate(split(jnp.transpose(got[...])), axis=0),
        chosen,
        preferred_element_type=f32,
    )
    lanes = 4 * CAP * PARTS
    spread = spread[:lanes] + spread[lanes:]
    slot = lax.broadcasted_iota(jnp.int32, (PARTS, NX), 1) % CAP
    loads = []
    for g in range(4):
        value = jnp.zeros((PARTS, NX), f32)
        for i in range(CAP):
            at = (g * CAP + i) * PARTS
            value = jnp.where(slot == i, spread[at : at + PARTS], value)
        loads.append(value)
    for k in range(2):
        at = k * STEPS
        report_out[k] = expected[pl.ds(at, STEPS), :] + loads[3][at : at + STEPS]
    place = lax.broadcasted_iota(jnp.int32, (PARTS, NX), 0)
    first = lower_half()
    transposed = (((1,), (1,)), ((), ()))

    def field(report, load, j, rows):
        tiles = code_tiles(rows)
        count = 8 * len(tiles)
        windows = []
        for k in range(2):
            n = k * STEPS + j
            code, column = decode(report[0, n : n + 1])
            a, b = report[1, n : n + 1], report[2, n : n + 1]
            weight = load[n : n + 1]
            parts = []
            for share in ((1.0 - a) * weight, a * weight):
                own, following = (1.0 - b) * share, b * share
                block = []
                for t in tiles:
                    tile = jnp.where(code == place + (8 * t - LEVELS), following, 0.0)
                    block.append(jnp.where(code == place + 8 * t, own, tile))
                parts += list(split(jnp.concatenate(block, axis=0)))
            out = lax.dot_general(
                jnp.concatenate(parts, axis=0),
                one_hot_columns(column),
                transposed,
                preferred_element_type=f32,
            )
            total = out[:count] + out[count : 2 * count]
            total = total + west(out[2 * count : 3 * count] + out[3 * count :])
            windows.append(total)
        for at, t in enumerate(tiles):
            one, two = (w[8 * at : 8 * at + 8] for w in windows)
            v, r = t // (STRIP // 2), 2 * (t % (STRIP // 2))
            yield v, r, jnp.where(first, one, pltpu.roll(two, LEVELS, 0))
            yield v, r + 1, jnp.where(first, pltpu.roll(one, LEVELS, 0), two)

    for j in range(STEPS):
        base = FIRST_FIELD[j]
        for v, r, tile in field(rep, loads[1], j, list(range(STRIP))):
            fields[base + v * (STRIP + 2 * j) + j + r] = tile
        if j > 0:
            for v, r, tile in field(sides.at[0], loads[0], j, list(range(STRIP - j, STRIP))):
                if r >= STRIP - j:
                    fields[base + v * (STRIP + 2 * j) + j + r - STRIP] = tile
            for v, r, tile in field(sides.at[1], loads[2], j, list(range(j))):
                if r < j:
                    fields[base + v * (STRIP + 2 * j) + j + r + STRIP] = tile
    for copy in copies:
        copy.wait()
    for c in range(PARTS):
        model = raw[0, c] * mult_out[c] + raw[1, c]
        model_out[c] = model if c < LEVELS else model - final0[c - LEVELS]


def adjoint_kernel(
    mult, outer, mine, outermost, back, fields,
    image,
    state, flux,
):
    def backdrop(v, row):
        if v > 0 and row in (0, EXT - 1):
            return outermost[v - 1, 1 if row else 0]
        return back[v, row]

    first = lower_half()
    half = EXT // 2
    for v in range(VARS):
        for i in range(half):
            own, after = mine[v * half + i], outer[v * half + i]
            state[0, v, i] = -jnp.where(first, own, pltpu.roll(after, LEVELS, 0))
            state[0, v, i + half] = -jnp.where(first, pltpu.roll(own, LEVELS, 0), after)
    weights = mix_weights(SCALE * coupling.T)
    for step, j in enumerate(reversed(range(STEPS))):
        now, later = state.at[step % 2], state.at[(step + 1) % 2]

        def added(v, row):
            return fields[FIRST_FIELD[j] + v * (STRIP + 2 * j) + row - step - 1]

        adjoint_step(step, now, later, backdrop, flux, weights, added)
    last = STEPS % 2
    for v in range(VARS):
        image[:, v] = mult[:, v] + state_rows(state[last, v, HALO : HALO + STRIP])


def finish_kernel(
    image, report, model, incoming, image_out, report_out, model_out, first, sems
):
    copies = [
        pltpu.make_async_copy(image, image_out, sems.at[0]),
        pltpu.make_async_copy(model.at[LEVELS:], model_out.at[LEVELS:], sems.at[1]),
        pltpu.make_async_copy(report, report_out, sems.at[2]),
        pltpu.make_async_copy(first, model_out.at[:LEVELS], sems.at[3]),
    ]
    for copy in copies[:3]:
        copy.start()
    first[...] = model[:LEVELS] - incoming[...]
    copies[3].start()
    for copy in copies:
        copy.wait()


def vmem(count):
    return [pl.BlockSpec(memory_space=pltpu.VMEM)] * count


def hbm(count):
    return [pl.BlockSpec(memory_space=pltpu.HBM)] * count


def far_from_core(x):
    return pltpu.with_memory_space_constraint(x, pltpu.HBM)


def shaped(*shape, kind=f32):
    return jax.ShapeDtypeStruct(shape, kind)


def cost(kernel_us):
    return pl.CostEstimate(flops=int(kernel_us * 1e9), bytes_accessed=int(kernel_us * 3e6), transcendentals=0)


def per_device(
    multipliers,
    increments,
    background,
    error_variance,
    report_weights,
    report_variance,
    report_cells,
    report_offsets,
    report_counts,
):
    mult, inc, bg, variance = (
        x.reshape(PARTS, VARS, STRIP, NX)
        for x in (multipliers, increments, background, error_variance)
    )
    count = lax.axis_size("space")
    wins = lax.axis_size("win")
    tile = (PARTS, NX)
    rows = shaped(VARS, STRIP, *tile)
    extended = shaped(VARS, EXT, *tile)
    whole = shaped(PARTS, VARS, STRIP, NX)
    scratch = pltpu.VMEM(whole.shape, f32)
    near, inner, rep, inc_rows, bg_rows, mult_rows = pl.pallas_call(
        pack_kernel,
        name="pack",
        out_shape=(
            shaped(NEAR, *tile),
            shaped(NEAR + FAR, *tile),
            shaped(3, *tile),
            rows,
            rows,
            rows,
        ),
        in_specs=hbm(6),
        out_specs=vmem(6),
        scratch_shapes=[
            pltpu.VMEM((3, *whole.shape), f32),
            pltpu.VMEM(report_cells.shape, jnp.int32),
            pltpu.VMEM(report_offsets.shape, f32),
            pltpu.VMEM(report_counts.shape, jnp.int32),
            pltpu.SemaphoreType.DMA((6,)),
        ],
        compiler_params=params,
    )(
        *(
            far_from_core(x)
            for x in (inc, bg, mult, report_cells, report_offsets, report_counts)
        )
    )
    both = lambda pairs: pairs + [(target, source) for source, target in pairs]
    near = lax.ppermute(near, "space", both([(i, i + 1) for i in range(1, count - 1, 2)]))
    inner = lax.ppermute(inner, "space", both([(i, i + 1) for i in range(0, count, 2)]))
    hot = shaped(2 * STEPS, NX, NX, kind=bf16)
    far, along, rests, early, known = pl.pallas_call(
        prepare_kernel,
        name="prepare",
        out_shape=(
            shaped(FAR, *tile), hot, hot, shaped(*tile), shaped(STEPS - 1, VARS, STRIP, *tile)
        ),
        in_specs=vmem(4),
        out_specs=vmem(5),
        scratch_shapes=[pltpu.VMEM((EXT, *tile), f32)],
        cost_estimate=cost(2),
        compiler_params=params,
    )(inc_rows, bg_rows, mult_rows, rep)
    far = lax.ppermute(far, "space", both([(i, i + 1) for i in range(1, count - 1, 2)]))
    final0, final1, send, expected, back = pl.pallas_call(
        tangent_kernel,
        name="tangent",
        out_shape=(
            shaped(LEVELS, VARS, STRIP, NX),
            shaped(LEVELS, VARS, STRIP, NX),
            shaped(OWNERS, 4 * CAP * PARTS),
            shaped(*tile),
            extended,
        ),
        in_specs=vmem(11),
        out_specs=vmem(2) + hbm(1) + vmem(2),
        scratch_shapes=[
            pltpu.VMEM((STEPS + 1, *extended.shape), f32),
            pltpu.VMEM((EXT, *tile), f32),
            pltpu.VMEM(tile, f32),
            pltpu.VMEM((OWNERS, 4 * CAP * PARTS), f32),
            pltpu.SemaphoreType.DMA,
        ],
        cost_estimate=cost(2),
        compiler_params=params,
    )(
        inc_rows, bg_rows, rep, along, rests, early, known, inner, near, report_weights,
        report_variance,
    )
    got = lax.all_to_all(send, "space", split_axis=0, concat_axis=0, tiled=True)
    folded = shaped(VARS * EXT // 2, *tile)
    half = shaped(LEVELS, VARS, STRIP, NX)
    outer, final1, mine, outermost, sides = pl.pallas_call(
        outer_kernel,
        name="outer",
        out_shape=(
            folded, half, folded, shaped(2, 2, *tile), shaped(2, 3, *tile)
        ),
        in_specs=vmem(4),
        out_specs=vmem(5),
        cost_estimate=cost(OUTER_COST),
        compiler_params=params,
    )(mult_rows, inner, far, final1)
    incoming = lax.ppermute(final1, "win", [(i, i + 1) for i in range(wins - 1)])
    outer = lax.ppermute(outer, "win", [(i + 1, i) for i in range(wins - 1)])
    report, fields, mult_near, model = pl.pallas_call(
        fields_kernel,
        name="fields",
        out_shape=(
            shaped(2, STEPS, NX), shaped(FIRST_FIELD[STEPS], *tile), whole, whole
        ),
        in_specs=hbm(3) + vmem(5),
        out_specs=vmem(4),
        scratch_shapes=[pltpu.VMEM((2, *whole.shape), f32), pltpu.SemaphoreType.DMA((3,))],
        cost_estimate=cost(FIELDS_COST),
        compiler_params=params,
    )(
        *(far_from_core(x) for x in (mult, variance, inc)),
        got, expected, rep, sides, final0,
    )
    image = pl.pallas_call(
        adjoint_kernel,
        name="adjoint",
        out_shape=whole,
        in_specs=vmem(6),
        out_specs=vmem(1)[0],
        scratch_shapes=[
            pltpu.VMEM((2, *extended.shape), f32),
            pltpu.VMEM(extended.shape, f32),
        ],
        cost_estimate=cost(ADJOINT_COST),
        compiler_params=params,
    )(mult_near, outer, mine, outermost, back, fields)
    image, report, model = pl.pallas_call(
        finish_kernel,
        name="finish",
        out_shape=(whole, shaped(2, STEPS, NX), whole),
        in_specs=vmem(4),
        out_specs=hbm(3),
        scratch_shapes=[pltpu.VMEM(half.shape, f32), pltpu.SemaphoreType.DMA((4,))],
        compiler_params=params,
    )(image, report, model, incoming)
    return model.reshape(multipliers.shape), report, image.reshape(multipliers.shape)


def solution(mesh):
    state = P("win", None, "space", None)
    slots = P("win", None, "space")
    return jax.shard_map(
        per_device,
        mesh=mesh,
        in_specs=(state, state, state, state, slots, slots, slots, P("win", None, None, "space"), slots),
        out_specs=(state, slots, state),
        check_vma=False,
    )
```
